256 devices in a mesh: expert: 128 (over z, x, y), dp: 2 (over core).
Axes of the slice: x: 4, y: 4, z: 8, core: 2. Of those that a mesh axis runs over, the one named last changes fastest.
Arguments:
- tokens: bfloat16 [32768, 2048], P(('dp', 'expert')), parts along dimension 0, may hold values from -24 to 24
- logits: float32 [32768, 128], P(('dp', 'expert')), parts along dimension 0, may hold values from -4 to 350
- weights: bfloat16 [128, 2048, 1024], P('expert'), may hold values from -0.125 to 0.125
- router_weight: bfloat16 [2048, 128], replicated, may hold values from -0.125 to 0.125
- expert_picks: int32 [256, 256], P(('dp', 'expert')), parts along dimension 0, may hold values from 0 to 16383, as said below
- cotangent: bfloat16 [256, 256, 1024], P(('dp', 'expert')), parts along dimension 0, may hold values from -1.5 to 1.5
Outputs:
- token_grad: bfloat16 [32768, 2048], P(('dp', 'expert')), parts along dimension 0
- weight_grad: bfloat16 [256, 2048, 1024], P(('dp', 'expert')), parts along dimension 0
- router_grad: float32 [4096, 128], P(('dp', 'expert')), parts along dimension 0
The draws below stay inside these ranges and needn't reach their ends.
There are 2 independent parts, one for each index of `dp`. The reference program is written for one: setup_inputs(seed, part) draws one part's arguments, and reference() takes and returns one part's arrays. A program takes and returns all parts, laid end to end along the dimension named above; an argument that names none is the same for every part. Nothing has to cross between parts.
Inputs may be any that keep to these rules, and one draw needn't show every extreme that they name: `expert_picks`: each expert's list is ascending and names no token twice. Among the tokens of one device (indices k * 128 to (k + 1) * 128 - 1) an expert takes at most 4, and in every draw each expert takes exactly 4 from some devices' tokens.
All inputs are finite; a program needn't handle non-finite values.
Results may differ from the reference program's by a relative error of at most 0.0062.
Values may be sent and summed in bfloat16 or wider, within the bound.
No kernel may reach another device: no remote copies, remote signals or barrier semaphores. Data moves between devices by JAX's collectives and lax.ppermute only.
A program may use at most 64 MiB of HBM per device.

```python
import jax
import jax.numpy as jnp
from jax import lax

D = 2048
H = 1024
TOK_DEV = 128
EXPERTS = 128
TOKENS = 16384
CAP = 256
MOST = 4


def shuffle_owners(key_one):
    return jax.random.permutation(key_one, EXPERTS)


def shuffle_tokens(key_one):
    return jax.random.permutation(key_one, TOK_DEV)


def scatter_list(target_pos, token_vals):
    return jnp.zeros((CAP,), jnp.int32).at[target_pos.reshape(-1)].set(token_vals.reshape(-1), mode='drop')


def choose_picks(key):
    key_hot, key_score, key_tie, key_rows = jax.random.split(key, 4)
    per_owner = CAP // EXPERTS
    owner_heat = jax.random.randint(key_hot, (1, EXPERTS), 0, 4)
    jitter = jax.random.randint(key_score, (EXPERTS, EXPERTS), 0, 8)
    tie_break = jax.vmap(shuffle_owners)(jax.random.split(key_tie, EXPERTS)).astype(jnp.int32)
    score = (owner_heat * 8 + jitter) * EXPERTS + tie_break
    ranked = jnp.argsort(-score, axis=1)
    rank_of = jnp.argsort(ranked, axis=1)
    counts = jnp.where(rank_of < EXPERTS // 4, 2 * per_owner, jnp.where(rank_of < 3 * EXPERTS // 4, per_owner, 0))
    starts = jnp.cumsum(counts, axis=1) - counts
    shuffled = jax.vmap(shuffle_tokens)(jax.random.split(key_rows, EXPERTS * EXPERTS)).astype(jnp.int32)
    chosen = jnp.sort(shuffled[:, :MOST], axis=1).reshape(EXPERTS, EXPERTS, MOST)
    columns = jnp.arange(MOST, dtype=jnp.int32)[None, None, :]
    owners = jnp.arange(EXPERTS, dtype=jnp.int32)[None, :, None]
    target = jnp.where(columns < counts[:, :, None], starts[:, :, None] + columns, CAP)
    token_ids = owners * TOK_DEV + chosen
    return jax.vmap(scatter_list)(target, token_ids).astype(jnp.int32)


def draw_expert_picks(key, part):
    return choose_picks(key)


def draw_logits(key, part):
    picks_now = choose_picks(key)
    key = jax.random.fold_in(key, 5)
    key_base = jax.random.fold_in(key, 0)
    picked = jnp.zeros((TOKENS, EXPERTS), jnp.float32).at[picks_now, jnp.arange(EXPERTS)[:, None]].set(1.0)
    base_logits = jnp.clip(jax.random.normal(key_base, (TOKENS, EXPERTS), jnp.float32), -4.0, 4.0)
    scores = base_logits + 5.0 * picked
    return scores.astype(jnp.float32)


def spiked(drawn, stream_key, source, target, parts, factor):
    def block_of(dim):
        return (jnp.arange(drawn.shape[dim]) // (drawn.shape[dim] // parts)).reshape((-1,) + (1,) * (drawn.ndim - 1 - dim))

    one_side = jax.random.permutation(stream_key, parts)[block_of(target)]
    other_side = (block_of(target) + parts // 2) % parts
    return jnp.where((block_of(source) == one_side) | (block_of(source) == other_side), factor * drawn, drawn)


def steps_of(stream_key, shape, shards, least, top_value):
    level = 1.0
    for position, blocks in shards:
        heights = jax.random.uniform(jax.random.fold_in(jax.random.fold_in(stream_key, 6), position), (blocks,), jnp.float32, least / len(shards), top_value / len(shards))
        level = level * jnp.repeat(jnp.exp(heights), shape[position] // blocks).reshape((-1,) + (1,) * (len(shape) - 1 - position))
    return level


def noise(own_key, dims, scale, most, shards=(), kind=jnp.bfloat16):
    drawn = scale * jax.random.normal(own_key, dims, jnp.float32)
    if shards:
        drawn = drawn * steps_of(own_key, dims, shards, -0.22, 0.18)
    return jnp.clip(drawn, -most, most).astype(kind)


def gaussian_with(key, shape, deviation, bound, pieces, heavy, kind=jnp.bfloat16):
    entries = deviation * jax.random.normal(key, shape, jnp.float32)
    if pieces:
        entries = entries * steps_of(key, shape, pieces, -0.22, 0.18)
    return jnp.clip(spiked(entries, jax.random.fold_in(key, 3), *heavy), -bound, bound).astype(kind)


def setup_inputs(seed: int = 0, part: int = 0) -> dict:
    keys = jax.random.split(jax.random.key(seed), 7)
    part_keys = jax.random.split(jax.random.fold_in(keys[6], part), 7)
    return {
        "tokens": gaussian_with(part_keys[0], (TOKENS, D), 1.0, 24.0, ((0, 128),), (0, 1, 128, 5.5)),
        "logits": draw_logits(jax.random.fold_in(jax.random.fold_in(keys[6], part), 71), part),
        "weights": noise(keys[2], (EXPERTS, D, H), D ** -0.5, 0.125, ((0, 128),)),
        "router_weight": noise(keys[3], (D, EXPERTS), D ** -0.5, 0.125),
        "expert_picks": draw_expert_picks(jax.random.fold_in(jax.random.fold_in(keys[6], part), 71), part),
        "cotangent": noise(part_keys[5], (EXPERTS, CAP, H), 0.25, 1.5, ((0, 128),)),
    }


def reference(tokens, logits, weights, router_weight, expert_picks, cotangent):
    gate_probs = jax.nn.softmax(logits, axis=-1)
    gate_table = lax.optimization_barrier(gate_probs.astype(jnp.bfloat16))
    width = tokens.shape[1]

    def one_expert(running, inputs):
        expert_part, score_grad = running
        weight, wanted, upstream, expert_id = inputs
        picked_rows = jnp.take(tokens, wanted, axis=0)
        gate_vals = gate_table[wanted, expert_id].astype(jnp.float32)
        active = jnp.dot(picked_rows, weight, preferred_element_type=jnp.float32)
        gate_grad = jnp.sum(upstream.astype(jnp.float32) * active, axis=1).astype(jnp.bfloat16)
        gate_grad = lax.optimization_barrier(gate_grad).astype(jnp.float32)
        scaled = (gate_vals[:, None] * upstream.astype(jnp.float32)).astype(jnp.bfloat16)
        weight_grad = lax.dot_general(picked_rows, scaled, (((0,), (0,)), ((), ())), preferred_element_type=jnp.float32).astype(jnp.bfloat16)
        row_grad = lax.dot_general(scaled, weight, (((1,), (1,)), ((), ())), preferred_element_type=jnp.float32).astype(jnp.bfloat16)
        row_grad = lax.optimization_barrier(row_grad).astype(jnp.float32)
        expert_part = expert_part.at[wanted].add(row_grad)
        score_grad = score_grad.at[wanted, expert_id].add(gate_grad)
        return (expert_part, score_grad), weight_grad

    start = (jnp.zeros((TOKENS, width), jnp.float32), jnp.zeros((TOKENS, EXPERTS), jnp.float32))
    (expert_part, score_grad), weight_grad = lax.scan(one_expert, start, (weights, expert_picks, cotangent, jnp.arange(EXPERTS, dtype=jnp.int32)))
    inner_sum = jnp.sum(gate_probs * score_grad, axis=1, keepdims=True)
    logit_grad = (gate_probs * (score_grad - inner_sum)).astype(jnp.bfloat16)
    router_part = lax.dot_general(logit_grad, router_weight, (((1,), (1,)), ((), ())), preferred_element_type=jnp.float32)
    token_grad = (expert_part + router_part).astype(jnp.bfloat16)
    router_grad = lax.dot_general(tokens, logit_grad, (((0,), (0,)), ((), ())), preferred_element_type=jnp.float32)
    return (token_grad, weight_grad, router_grad)
```

```python
import jax
import jax.numpy as jnp
from jax import lax
from jax.sharding import PartitionSpec as P

F32 = jnp.float32
BF16 = jnp.bfloat16


def matmul(a, b, dims):
    return lax.dot_general(a, b, (dims, ((), ())), preferred_element_type=F32)


def exchange(x):
    return lax.all_to_all(x, "expert", split_axis=0, concat_axis=0, tiled=True)


def local(tokens, logits, weights, router_weight, expert_picks, cotangent):
    experts = lax.axis_size("expert")
    tok_rows, width = tokens.shape
    capacity = expert_picks.shape[1]
    most = 2 * capacity // experts
    slots = experts * most
    weight, upstream, wanted = weights[0], cotangent[0], expert_picks[0]

    owners = wanted // tok_rows
    rank = jnp.zeros_like(owners)
    for back in range(1, most):
        rank = rank + jnp.pad((owners[back:] == owners[:-back]).astype(jnp.int32), (back, 0))
    placed = owners * most + rank
    place = jnp.arange(slots, dtype=jnp.int32)[:, None] == placed[None, :]
    ids = jnp.sum(jnp.where(place, (wanted % tok_rows)[None, :] + 1, 0), axis=1) - 1
    requested = exchange(ids.reshape(experts, most)).reshape(slots)
    up_slots = matmul(place.astype(BF16), upstream, ((1,), (0,))).astype(BF16)
    raw_grad = matmul(up_slots, weight, ((1,), (1,))).astype(BF16)
    got_raw = exchange(raw_grad.reshape(experts, most, width)).reshape(slots, width)

    probs = jax.nn.softmax(logits, axis=-1)
    chosen = jnp.arange(tok_rows, dtype=jnp.int32)[:, None] == requested[None, :]
    slot_ids = jnp.arange(slots, dtype=jnp.int32)
    of_expert = slot_ids[:, None] // most == jnp.arange(experts, dtype=jnp.int32)[None, :]
    of_expert = of_expert.astype(BF16)
    gates = matmul(probs.astype(BF16), of_expert, ((1,), (1,)))
    gated = jnp.where(chosen, gates, 0.0).astype(BF16)
    send_rows = matmul(gated, tokens, ((0,), (0,))).astype(BF16)
    got_rows = exchange(send_rows.reshape(experts, most, width)).reshape(slots, width)

    products = matmul(tokens, got_raw, ((1,), (1,)))
    picked = jnp.where(chosen, products, 0.0).astype(BF16)
    score_grad = matmul(picked, of_expert, ((1,), (0,)))
    inner_sum = jnp.sum(probs * score_grad, axis=1, keepdims=True)
    logit_grad = (probs * (score_grad - inner_sum)).astype(BF16)
    router_part = matmul(tokens, logit_grad, ((0,), (0,)))
    shares = exchange(router_part.reshape(experts, width // experts, experts))
    token_grad = (
        matmul(gated, got_raw, ((1,), (0,))) + matmul(logit_grad, router_weight, ((1,), (1,)))
    ).astype(BF16)

    weight_grad = matmul(got_rows, up_slots, ((0,), (0,))).astype(BF16)
    router_grad = jnp.sum(shares, axis=0)
    return (token_grad, weight_grad[None], router_grad)


def solution(mesh):
    in_specs = (
        P(("dp", "expert"), None),
        P(("dp", "expert"), None),
        P("expert", None, None),
        P(),
        P(("dp", "expert"), None),
        P(("dp", "expert"), None, None),
    )
    out_specs = (
        P(("dp", "expert"), None),
        P(("dp", "expert"), None, None),
        P(("dp", "expert"), None),
    )
    return jax.shard_map(local, mesh=mesh, in_specs=in_specs, out_specs=out_specs, check_vma=False)
```

```python
import jax
import jax.numpy as jnp
from jax import lax
from jax.sharding import PartitionSpec as P

F32 = jnp.float32
BF16 = jnp.bfloat16
LANES = 128
SIDES = (8, 4, 4)


def matmul(a, b, dims):
    return lax.dot_general(a, b, (dims, ((), ())), preferred_element_type=F32)


def exchange(x):
    return lax.all_to_all(x, "expert", split_axis=0, concat_axis=0, tiled=True)


def sum_shares(parts):
    index = lax.axis_index("expert")
    count = lax.axis_size("expert")
    for side in (2, 1, 0):
        size = SIDES[side]
        stride = 1
        for later in SIDES[side + 1 :]:
            stride *= later
        here = index // stride % size

        def pick(step):
            return lax.dynamic_index_in_dim(parts, (here + step) % size, side, keepdims=False)

        def moved(i, step):
            at = i // stride % size
            return i + ((at + step) % size - at) * stride

        total = pick(0)
        for step in range(1, size):
            total = total + lax.ppermute(
                pick(step), "expert", [(i, moved(i, step)) for i in range(count)]
            )
        parts = total
    return parts


def local(tokens, logits, weights, router_weight, expert_picks, cotangent):
    experts = lax.axis_size("expert")
    tok_rows, width = tokens.shape
    capacity = expert_picks.shape[1]
    most = 2 * capacity // experts
    slots = experts * most
    weight, upstream, wanted = weights[0], cotangent[0], expert_picks[0]

    owners = wanted // tok_rows
    rank = jnp.zeros_like(owners)
    for back in range(1, most):
        rank = rank + jnp.pad((owners[back:] == owners[:-back]).astype(jnp.int32), (back, 0))
    placed = owners * most + rank
    place = jnp.arange(slots, dtype=jnp.int32)[:, None] == placed[None, :]
    ids = jnp.sum(jnp.where(place, (wanted % tok_rows)[None, :] + 1, 0), axis=1)
    up_slots = matmul(place.astype(BF16), upstream, ((1,), (0,))).astype(BF16)
    raw_grad = matmul(up_slots, weight, ((1,), (1,))).astype(BF16)
    marks = jnp.broadcast_to(ids.astype(BF16).reshape(experts, most, 1), (experts, most, LANES))
    got = exchange(jnp.concatenate([raw_grad.reshape(experts, most, width), marks], axis=2))
    got_raw = got[:, :, :width].reshape(slots, width)
    requested = got[:, :, width].astype(jnp.int32).reshape(slots) - 1

    probs = jax.nn.softmax(logits, axis=-1)
    chosen = jnp.arange(tok_rows, dtype=jnp.int32)[:, None] == requested[None, :]
    slot_ids = jnp.arange(slots, dtype=jnp.int32)
    of_expert = slot_ids[:, None] // most == jnp.arange(experts, dtype=jnp.int32)[None, :]
    of_expert = of_expert.astype(BF16)
    gates = matmul(probs.astype(BF16), of_expert, ((1,), (1,)))
    gated = jnp.where(chosen, gates, 0.0).astype(BF16)
    send_rows = matmul(gated, tokens, ((0,), (0,))).astype(BF16)
    got_rows = exchange(send_rows.reshape(experts, most, width)).reshape(slots, width)

    products = matmul(tokens, got_raw, ((1,), (1,)))
    picked = jnp.where(chosen, products, 0.0).astype(BF16)
    score_grad = matmul(picked, of_expert, ((1,), (0,)))
    inner_sum = jnp.sum(probs * score_grad, axis=1, keepdims=True)
    logit_grad = (probs * (score_grad - inner_sum)).astype(BF16)
    router_part = matmul(tokens, logit_grad, ((0,), (0,)))
    router_grad = sum_shares(router_part.reshape(*SIDES, width // experts, experts))
    token_grad = (
        matmul(gated, got_raw, ((1,), (0,))) + matmul(logit_grad, router_weight, ((1,), (1,)))
    ).astype(BF16)

    weight_grad = matmul(got_rows, up_slots, ((0,), (0,))).astype(BF16)
    return (token_grad, weight_grad[None], router_grad)


def solution(mesh):
    in_specs = (
        P(("dp", "expert"), None),
        P(("dp", "expert"), None),
        P("expert", None, None),
        P(),
        P(("dp", "expert"), None),
        P(("dp", "expert"), None, None),
    )
    out_specs = (
        P(("dp", "expert"), None),
        P(("dp", "expert"), None, None),
        P(("dp", "expert"), None),
    )
    return jax.shard_map(local, mesh=mesh, in_specs=in_specs, out_specs=out_specs, check_vma=False)
```

```python
import jax
import jax.numpy as jnp
from jax import lax
from jax.sharding import PartitionSpec as P

F32 = jnp.float32
BF16 = jnp.bfloat16
LANES = 128
SIDES = (8, 4, 4)


def matmul(a, b, dims):
    return lax.dot_general(a, b, (dims, ((), ())), preferred_element_type=F32)


def exchange(x):
    return lax.all_to_all(x, "expert", split_axis=0, concat_axis=0, tiled=True)


def sum_shares(parts):
    index = lax.axis_index("expert")
    count = lax.axis_size("expert")
    for side in (2, 1, 0):
        size = SIDES[side]
        stride = 1
        for later in SIDES[side + 1 :]:
            stride *= later
        here = index // stride % size

        def pick(step):
            return lax.dynamic_index_in_dim(parts, (here + step) % size, side, keepdims=False)

        def moved(i, step):
            at = i // stride % size
            return i + ((at + step) % size - at) * stride

        total = pick(0)
        for step in range(1, size):
            total = total + lax.ppermute(
                pick(step), "expert", [(i, moved(i, step)) for i in range(count)]
            )
        parts = total
    return parts


def local(tokens, logits, weights, router_weight, expert_picks, cotangent):
    experts = lax.axis_size("expert")
    tok_rows, width = tokens.shape
    capacity = expert_picks.shape[1]
    most = 2 * capacity // experts
    slots = experts * most
    weight, upstream, wanted = weights[0], cotangent[0], expert_picks[0]

    def expert_side():
        owners = wanted // tok_rows
        rank = jnp.zeros_like(owners)
        for back in range(1, most):
            rank = rank + jnp.pad((owners[back:] == owners[:-back]).astype(jnp.int32), (back, 0))
        placed = owners * most + rank
        place = jnp.arange(slots, dtype=jnp.int32)[:, None] == placed[None, :]
        ids = jnp.sum(jnp.where(place, (wanted % tok_rows)[None, :] + 1, 0), axis=1)
        up_slots = matmul(place.astype(BF16), upstream, ((1,), (0,))).astype(BF16)
        raw_grad = matmul(up_slots, weight, ((1,), (1,))).astype(BF16)
        return ids, up_slots, raw_grad.reshape(experts, most, width)

    def gated_rows(requested):
        probs = jax.nn.softmax(logits, axis=-1)
        chosen = jnp.arange(tok_rows, dtype=jnp.int32)[:, None] + 1 == requested[None, :]
        slot_ids = jnp.arange(slots, dtype=jnp.int32)
        of_expert = slot_ids[:, None] // most == jnp.arange(experts, dtype=jnp.int32)[None, :]
        of_expert = of_expert.astype(BF16)
        gates = matmul(probs.astype(BF16), of_expert, ((1,), (1,)))
        gated = jnp.where(chosen, gates, 0.0).astype(BF16)
        rows = matmul(gated, tokens, ((0,), (0,))).astype(BF16).reshape(experts, most, width)
        return probs, chosen, of_expert, gated, rows

    def owner_side(got_raw, probs, chosen, of_expert, gated):
        products = matmul(tokens, got_raw, ((1,), (1,)))
        picked = jnp.where(chosen, products, 0.0).astype(BF16)
        score_grad = matmul(picked, of_expert, ((1,), (0,)))
        inner_sum = jnp.sum(probs * score_grad, axis=1, keepdims=True)
        logit_grad = (probs * (score_grad - inner_sum)).astype(BF16)
        router_part = matmul(tokens, logit_grad, ((0,), (0,)))
        router_grad = sum_shares(router_part.reshape(*SIDES, width // experts, experts))
        token_grad = (
            matmul(gated, got_raw, ((1,), (0,))) + matmul(logit_grad, router_weight, ((1,), (1,)))
        ).astype(BF16)
        return token_grad, router_grad

    def finish(got_rows, up_slots):
        return matmul(got_rows.reshape(slots, width), up_slots, ((0,), (0,))).astype(BF16)[None]

    def ids_inside():
        ids, up_slots, raw_grad = expert_side()
        marks = jnp.broadcast_to(ids.astype(BF16).reshape(experts, most, 1), (experts, most, LANES))
        got = exchange(jnp.concatenate([raw_grad, marks], axis=2))
        requested = got[:, :, width].astype(jnp.int32).reshape(slots)
        *known, rows = gated_rows(requested)
        got_rows = exchange(rows)
        token_grad, router_grad = owner_side(got[:, :, :width].reshape(slots, width), *known)
        return token_grad, finish(got_rows, up_slots), router_grad

    def ids_first():
        ids, up_slots, raw_grad = expert_side()
        requested = exchange(ids.reshape(experts, most)).reshape(slots)
        got_raw = exchange(raw_grad).reshape(slots, width)
        *known, rows = gated_rows(requested)
        got_rows = exchange(rows)
        token_grad, router_grad = owner_side(got_raw, *known)
        return token_grad, finish(got_rows, up_slots), router_grad

    return lax.cond(lax.axis_index("dp") == 0, ids_inside, ids_first)


def solution(mesh):
    in_specs = (
        P(("dp", "expert"), None),
        P(("dp", "expert"), None),
        P("expert", None, None),
        P(),
        P(("dp", "expert"), None),
        P(("dp", "expert"), None, None),
    )
    out_specs = (
        P(("dp", "expert"), None),
        P(("dp", "expert"), None, None),
        P(("dp", "expert"), None),
    )
    return jax.shard_map(local, mesh=mesh, in_specs=in_specs, out_specs=out_specs, check_vma=False)
```

```python
import functools

import jax
import jax.numpy as jnp
from jax import lax
from jax.experimental import pallas as pl
from jax.experimental.pallas import tpu as pltpu
from jax.sharding import PartitionSpec as P

F32 = jnp.float32
BF16 = jnp.bfloat16
I32 = jnp.int32
LANES = 128
HALVES = 2
STEP = 256

NN = ((1,), (0,))
NT = ((1,), (1,))
TN = ((0,), (0,))


def matmul(a, b, dims):
    return lax.dot_general(a, b, (dims, ((), ())), preferred_element_type=F32)


def iota(shape, dim):
    return lax.broadcasted_iota(I32, shape, dim)


def params():
    return pltpu.CompilerParams(vmem_limit_bytes=40 * 1024 * 1024)


def slots_of(wanted, tok_rows, most):
    cap = wanted.shape[1]
    owners = jnp.broadcast_to(wanted // tok_rows, (8, cap))
    lane = iota((8, cap), 1)
    rank = jnp.zeros((8, cap), I32)
    for back in range(1, most):
        same = (pltpu.roll(owners, back, 1) == owners) & (lane >= back)
        rank = rank + same.astype(I32)
    return owners[:1], rank[:1], wanted % tok_rows + 1


def place_rows(rows, wanted, tok_rows, most):
    owners, rank, _ = slots_of(wanted, tok_rows, most)
    first = owners * (HALVES * most) + rank
    target = jnp.concatenate([first + half * most for half in range(HALVES)], axis=1)
    return iota((rows, target.shape[1]), 0) == target


def lists_kernel(tok_rows, most, picks_ref, out_ref):
    owners, rank, marks = slots_of(picks_ref[...], tok_rows, most)
    cap = owners.shape[1]
    rows = out_ref.shape[0]
    left = jnp.where(iota((rows, cap), 0) == owners, marks, 0).astype(F32).astype(BF16)
    right = (iota((LANES, cap), 0) == rank).astype(F32).astype(BF16)
    out_ref[...] = matmul(left, right, NT)


def raw_kernel(tok_rows, most, picks_ref, up_ref, weight_ref, out_ref, place_ref):
    step = pl.program_id(0)
    rows, cap = out_ref.shape[0], up_ref.shape[0]
    half_width = weight_ref.shape[1] * pl.num_programs(0)

    @pl.when(step == 0)
    def _():
        wanted = picks_ref[...]
        hot = place_rows(rows, wanted, tok_rows, most)
        place_ref[...] = hot.astype(F32).astype(BF16)
        if out_ref.shape[1] > half_width:
            marks = slots_of(wanted, tok_rows, most)[2]
            both = jnp.concatenate([marks] * HALVES, axis=1)
            named = jnp.where(hot, both, 0).astype(F32).astype(BF16)
            ones = jnp.ones((LANES, HALVES * cap), BF16)
            out_ref[:, half_width:] = matmul(named, ones, NT).astype(BF16)

    up = up_ref[...]
    parts = [matmul(up, weight_ref[half], NT).astype(BF16) for half in range(HALVES)]
    columns = pl.ds(pl.multiple_of(step * STEP, STEP), STEP)
    out_ref[:, columns] = matmul(place_ref[...], jnp.concatenate(parts, axis=0), NN).astype(BF16)


def split_halves(gated, most):
    half = iota(gated.shape, 0) // most % HALVES
    return jnp.concatenate(
        [jnp.where(half == h, gated, 0.0).astype(BF16) for h in range(HALVES)], axis=1
    )


def owner_kernel(most, lists, got_ref, marks_ref, tokens_ref, logits_ref, send_ref, gated_ref, grad_ref):
    rows = send_ref.shape[0]
    half_width = got_ref.shape[1]
    lane = iota((rows, LANES), 1)
    row = iota((rows, LANES), 0)
    of_expert = (row // (HALVES * most) == lane).astype(F32).astype(BF16)
    if lists:
        spread = matmul(of_expert, marks_ref[...].astype(BF16), NN)
        marks = jnp.sum(jnp.where(lane == row % most, spread, 0.0), axis=1, keepdims=True)
    else:
        marks = marks_ref[...].astype(F32)
    chosen = marks == (lane + 1).astype(F32)

    logits = logits_ref[...]
    raised = jnp.exp(logits - jnp.max(logits, axis=1, keepdims=True))
    probs = raised / jnp.sum(raised, axis=1, keepdims=True)
    gates = matmul(of_expert, probs.astype(BF16), NT)
    gated = jnp.where(chosen, gates, 0.0)
    gated_ref[...] = gated.astype(BF16)
    tokens = tokens_ref[...]
    stack = jnp.concatenate(
        [tokens[:, h * half_width : (h + 1) * half_width] for h in range(HALVES)], axis=0
    )
    send_ref[:, :half_width] = matmul(split_halves(gated, most), stack, NN).astype(BF16)

    products = matmul(got_ref[...], stack, NT)
    half = row // most % HALVES
    own = products[:, :LANES]
    for h in range(1, HALVES):
        own = jnp.where(half == h, products[:, h * LANES : (h + 1) * LANES], own)
    own = jnp.where(chosen, own, 0.0)
    whole = own + pltpu.roll(own, most, 0)
    gate_grad = jnp.where(half == HALVES - 1, whole, 0.0).astype(BF16)
    score_grad = matmul(gate_grad, of_expert, TN)
    inner_sum = jnp.sum(probs * score_grad, axis=1, keepdims=True)
    logit_grad = (probs * (score_grad - inner_sum)).astype(BF16)
    grad_ref[...] = logit_grad
    shares = matmul(tokens, logit_grad, TN)
    blocks = rows // 8
    shares = shares.reshape(blocks, 16, LANES)
    for b in range(2):
        part = shares[:, 8 * b : 8 * (b + 1), :].reshape(rows, LANES)
        send_ref[:, half_width + b * LANES : half_width + (b + 1) * LANES] = part.astype(BF16)


def token_kernel(most, got_ref, gated_ref, grad_ref, router_ref, out_ref):
    half_width = got_ref.shape[1]
    tok_rows = out_ref.shape[0]
    expert_part = matmul(split_halves(gated_ref[...].astype(F32), most), got_ref[...], TN)
    for h in range(HALVES):
        columns = slice(h * half_width, (h + 1) * half_width)
        router_part = matmul(grad_ref[...], router_ref[columns, :], NT)
        out_ref[:, columns] = (expert_part[h * tok_rows : (h + 1) * tok_rows] + router_part).astype(BF16)


def final_kernel(tok_rows, most, got_ref, shares_ref, picks_ref, up_ref, out_ref, router_ref, place_ref):
    rows, cap = got_ref.shape[0], up_ref.shape[0]
    chunk, half = pl.program_id(0), pl.program_id(1)

    @pl.when((chunk == 0) & (half == 0))
    def _():
        hot = place_rows(rows, picks_ref[...], tok_rows, most).astype(F32).astype(BF16)
        for h in range(HALVES):
            place_ref[h] = hot[:, h * cap : (h + 1) * cap]
        for b in range(2):
            part = shares_ref[:, b * LANES : (b + 1) * LANES].astype(F32)
            router_ref[8 * b : 8 * (b + 1), :] = jnp.sum(part.reshape(rows // 8, 8, LANES), axis=0)

    picked = matmul(place_ref[half], got_ref[...], TN).astype(BF16)
    out_ref[...] = matmul(picked, up_ref[...], TN).astype(BF16)


def exchange(x, blocks):
    x = x.reshape(blocks, x.shape[0] // blocks, x.shape[1])
    x = lax.all_to_all(x, "expert", split_axis=0, concat_axis=0, tiled=True)
    return x.reshape(-1, x.shape[2])


def local(tokens, logits, weights, router_weight, expert_picks, cotangent):
    experts = lax.axis_size("expert")
    tok_rows, width = tokens.shape
    hidden = weights.shape[2]
    cap = expert_picks.shape[1]
    most = 2 * cap // experts
    rows = experts * most * HALVES
    half_width = width // HALVES
    weight = weights[0].reshape(HALVES, half_width, hidden)
    upstream = cotangent[0]
    full = lambda *shape: pl.BlockSpec(shape, lambda *_: (0,) * len(shape))
    shape_of = jax.ShapeDtypeStruct

    def raw_grads(columns):
        return pl.pallas_call(
            functools.partial(raw_kernel, tok_rows, most),
            grid=(half_width // STEP,),
            in_specs=[
                full(1, cap),
                full(cap, hidden),
                pl.BlockSpec((HALVES, STEP, hidden), lambda i: (0, i, 0)),
            ],
            out_specs=full(rows, columns),
            out_shape=shape_of((rows, columns), BF16),
            scratch_shapes=[pltpu.VMEM((rows, HALVES * cap), BF16)],
            compiler_params=params(),
            name="raw_grads",
        )(expert_picks, upstream, weight)

    def owner_step(got, marks, lists):
        marks_spec = full(experts, LANES) if lists else pl.BlockSpec((rows, LANES), lambda i: (0, half_width // LANES))
        return pl.pallas_call(
            functools.partial(owner_kernel, most, lists),
            grid=(1,),
            in_specs=[pl.BlockSpec((rows, half_width), lambda i: (0, 0)), marks_spec, full(tok_rows, width), full(tok_rows, experts)],
            out_specs=[full(rows, half_width + 2 * LANES), full(rows, LANES), full(tok_rows, experts)],
            out_shape=[
                shape_of((rows, half_width + 2 * LANES), BF16),
                shape_of((rows, LANES), BF16),
                shape_of((tok_rows, experts), BF16),
            ],
            compiler_params=params(),
            name="owner_step",
        )(got, marks, tokens, logits)

    def token_step(got, gated, grad):
        return pl.pallas_call(
            functools.partial(token_kernel, most),
            grid=(1,),
            in_specs=[full(rows, half_width), full(rows, LANES), full(tok_rows, experts), full(width, experts)],
            out_specs=full(tok_rows, width),
            out_shape=shape_of((tok_rows, width), BF16),
            compiler_params=params(),
            cost_estimate=pl.CostEstimate(flops=10**9, bytes_accessed=4 * 10**6, transcendentals=0),
            name="token_step",
        )(got, gated, grad, router_weight)

    def final_step(got):
        chunks = 2
        piece = half_width // chunks
        return pl.pallas_call(
            functools.partial(final_kernel, tok_rows, most),
            grid=(chunks, HALVES),
            in_specs=[
                pl.BlockSpec((rows, piece), lambda i, h: (0, i)),
                pl.BlockSpec((rows, 2 * LANES), lambda i, h: (0, half_width // (2 * LANES))),
                full(1, cap),
                full(cap, hidden),
            ],
            out_specs=[
                pl.BlockSpec((piece, hidden), lambda i, h: (h * chunks + i, 0)),
                full(width // experts, experts),
            ],
            out_shape=[shape_of((width, hidden), BF16), shape_of((width // experts, experts), F32)],
            scratch_shapes=[pltpu.VMEM((HALVES, rows, cap), BF16)],
            compiler_params=params(),
            name="final_step",
        )(got, got, expert_picks, upstream)

    def rest(got, marks, lists):
        send, gated, grad = owner_step(got, marks, lists)
        got_rows = exchange(send, experts)
        token_grad = token_step(got, gated, grad)
        weight_grad, router_grad = final_step(got_rows)
        return token_grad, weight_grad[None], router_grad

    def ids_inside():
        got = exchange(raw_grads(half_width + LANES), experts)
        return rest(got, got, False)

    def ids_first():
        named = pl.pallas_call(
            functools.partial(lists_kernel, tok_rows, most),
            out_shape=shape_of((experts, LANES), F32),
            name="lists",
        )(expert_picks)
        lists = exchange(named, experts)
        return rest(exchange(raw_grads(half_width), experts), lists, True)

    return lax.cond(lax.axis_index("dp") == 0, ids_inside, ids_first)


def solution(mesh):
    in_specs = (
        P(("dp", "expert"), None),
        P(("dp", "expert"), None),
        P("expert", None, None),
        P(),
        P(("dp", "expert"), None),
        P(("dp", "expert"), None, None),
    )
    out_specs = (
        P(("dp", "expert"), None),
        P(("dp", "expert"), None, None),
        P(("dp", "expert"), None),
    )
    return jax.shard_map(local, mesh=mesh, in_specs=in_specs, out_specs=out_specs, check_vma=False)
```

```python
import functools

import jax
import jax.numpy as jnp
from jax import lax
from jax.experimental import pallas as pl
from jax.experimental.pallas import tpu as pltpu
from jax.sharding import PartitionSpec as P

F32 = jnp.float32
BF16 = jnp.bfloat16
I32 = jnp.int32
LANES = 128
HALVES = 2
STEP = 256

NN = ((1,), (0,))
NT = ((1,), (1,))
TN = ((0,), (0,))


def matmul(a, b, dims):
    return lax.dot_general(a, b, (dims, ((), ())), preferred_element_type=F32)


def iota(shape, dim):
    return lax.broadcasted_iota(I32, shape, dim)


def params(mebibytes=60):
    return pltpu.CompilerParams(vmem_limit_bytes=mebibytes * 1024 * 1024)


def slots_of(wanted, tok_rows, most):
    cap = wanted.shape[1]
    owners = jnp.broadcast_to(wanted // tok_rows, (8, cap))
    lane = iota((8, cap), 1)
    rank = jnp.zeros((8, cap), I32)
    for back in range(1, most):
        same = (pltpu.roll(owners, back, 1) == owners) & (lane >= back)
        rank = rank + same.astype(I32)
    return owners[:1], rank[:1], wanted % tok_rows + 1


def place_rows(rows, wanted, tok_rows, most):
    owners, rank, _ = slots_of(wanted, tok_rows, most)
    first = owners * (HALVES * most) + rank
    target = jnp.concatenate([first + half * most for half in range(HALVES)], axis=1)
    return iota((rows, target.shape[1]), 0) == target


def name_lists(wanted, owners_count, tok_rows, most):
    owners, rank, marks = slots_of(wanted, tok_rows, most)
    cap = owners.shape[1]
    left = jnp.where(iota((owners_count, cap), 0) == owners, marks, 0).astype(F32).astype(BF16)
    right = (iota((LANES, cap), 0) == rank).astype(F32).astype(BF16)
    return matmul(left, right, NT)


def raw_kernel(tok_rows, most, picks_ref, up_ref, weight_ref, out_ref, *rest):
    place_ref = rest[-1]
    step = pl.program_id(0)
    rows, cap = out_ref.shape[0], up_ref.shape[0]
    half_width = weight_ref.shape[1] * pl.num_programs(0)

    @pl.when(step == 0)
    def _():
        wanted = picks_ref[...]
        hot = place_rows(rows, wanted, tok_rows, most)
        place_ref[...] = hot.astype(F32).astype(BF16)
        if len(rest) > 1:
            rest[0][...] = name_lists(wanted, rest[0].shape[0], tok_rows, most)
        else:
            marks = slots_of(wanted, tok_rows, most)[2]
            both = jnp.concatenate([marks] * HALVES, axis=1)
            named = jnp.where(hot, both, 0).astype(F32).astype(BF16)
            ones = jnp.ones((LANES, HALVES * cap), BF16)
            out_ref[:, half_width:] = matmul(named, ones, NT).astype(BF16)

    up = up_ref[...]
    parts = [matmul(up, weight_ref[half], NT).astype(BF16) for half in range(HALVES)]
    columns = pl.ds(pl.multiple_of(step * STEP, STEP), STEP)
    out_ref[:, columns] = matmul(place_ref[...], jnp.concatenate(parts, axis=0), NN).astype(BF16)


def split_halves(gated, most):
    half = iota(gated.shape, 0) // most % HALVES
    return jnp.concatenate(
        [jnp.where(half == h, gated, 0.0).astype(BF16) for h in range(HALVES)], axis=1
    )


def owner_kernel(most, lists, got_ref, marks_ref, tokens_ref, logits_ref, send_ref, gated_ref, grad_ref):
    rows = send_ref.shape[0]
    half_width = got_ref.shape[1]
    lane = iota((rows, LANES), 1)
    row = iota((rows, LANES), 0)
    of_expert = (row // (HALVES * most) == lane).astype(F32).astype(BF16)
    if lists:
        spread = matmul(of_expert, marks_ref[...].astype(BF16), NN)
        marks = jnp.sum(jnp.where(lane == row % most, spread, 0.0), axis=1, keepdims=True)
    else:
        marks = marks_ref[...].astype(F32)
    chosen = marks == (lane + 1).astype(F32)

    logits = logits_ref[...]
    raised = jnp.exp(logits - jnp.max(logits, axis=1, keepdims=True))
    probs = raised / jnp.sum(raised, axis=1, keepdims=True)
    gates = matmul(of_expert, probs.astype(BF16), NT)
    gated = jnp.where(chosen, gates, 0.0)
    gated_ref[...] = gated.astype(BF16)
    tokens = tokens_ref[...]
    stack = jnp.concatenate(
        [tokens[:, h * half_width : (h + 1) * half_width] for h in range(HALVES)], axis=0
    )
    send_ref[:, :half_width] = matmul(split_halves(gated, most), stack, NN).astype(BF16)

    products = matmul(got_ref[...], stack, NT)
    half = row // most % HALVES
    own = products[:, :LANES]
    for h in range(1, HALVES):
        own = jnp.where(half == h, products[:, h * LANES : (h + 1) * LANES], own)
    own = jnp.where(chosen, own, 0.0)
    whole = own + pltpu.roll(own, most, 0)
    gate_grad = jnp.where(half == HALVES - 1, whole, 0.0).astype(BF16)
    score_grad = matmul(gate_grad, of_expert, TN)
    inner_sum = jnp.sum(probs * score_grad, axis=1, keepdims=True)
    logit_grad = (probs * (score_grad - inner_sum)).astype(BF16)
    grad_ref[...] = logit_grad
    shares = matmul(tokens, logit_grad, TN)
    blocks = rows // 8
    shares = shares.reshape(blocks, 16, LANES)
    for b in range(2):
        part = shares[:, 8 * b : 8 * (b + 1), :].reshape(rows, LANES)
        send_ref[:, half_width + b * LANES : half_width + (b + 1) * LANES] = part.astype(BF16)


def token_kernel(most, picks_ref, got_ref, gated_ref, grad_ref, router_ref, out_ref, place_ref):
    half_width = got_ref.shape[1]
    tok_rows = out_ref.shape[0]
    hot = place_rows(got_ref.shape[0], picks_ref[...], tok_rows, most)
    place_ref[...] = hot.astype(F32).T.astype(BF16)
    expert_part = matmul(split_halves(gated_ref[...].astype(F32), most), got_ref[...], TN)
    for h in range(HALVES):
        columns = slice(h * half_width, (h + 1) * half_width)
        router_part = matmul(grad_ref[...], router_ref[columns, :], NT)
        out_ref[:, columns] = (expert_part[h * tok_rows : (h + 1) * tok_rows] + router_part).astype(BF16)


def final_kernel(got_ref, shares_ref, place_ref, up_ref, out_ref, router_ref):
    rows, cap = got_ref.shape[0], up_ref.shape[0]
    chunk, half = pl.program_id(0), pl.program_id(1)

    @pl.when((chunk == 0) & (half == 0))
    def _():
        for b in range(2):
            part = shares_ref[:, b * LANES : (b + 1) * LANES].astype(F32)
            router_ref[8 * b : 8 * (b + 1), :] = jnp.sum(part.reshape(rows // 8, 8, LANES), axis=0)

    picks = pl.ds(pl.multiple_of(half * cap, cap), cap)
    picked = matmul(place_ref[picks, :], got_ref[...], NN).astype(BF16)
    out_ref[...] = matmul(picked, up_ref[...], TN).astype(BF16)


def exchange(x, blocks):
    x = x.reshape(blocks, x.shape[0] // blocks, x.shape[1])
    x = lax.all_to_all(x, "expert", split_axis=0, concat_axis=0, tiled=True)
    return x.reshape(-1, x.shape[2])


def local(tokens, logits, weights, router_weight, expert_picks, cotangent):
    experts = lax.axis_size("expert")
    tok_rows, width = tokens.shape
    hidden = weights.shape[2]
    cap = expert_picks.shape[1]
    most = 2 * cap // experts
    rows = experts * most * HALVES
    half_width = width // HALVES
    weight = weights[0].reshape(HALVES, half_width, hidden)
    upstream = cotangent[0]
    full = lambda *shape: pl.BlockSpec(shape, lambda *_: (0,) * len(shape))
    shape_of = jax.ShapeDtypeStruct

    def raw_grads(lists):
        columns = half_width if lists else half_width + LANES
        out = pl.pallas_call(
            functools.partial(raw_kernel, tok_rows, most),
            grid=(half_width // STEP,),
            in_specs=[
                full(1, cap),
                full(cap, hidden),
                pl.BlockSpec((HALVES, STEP, hidden), lambda i: (0, i, 0)),
            ],
            out_specs=[full(rows, columns)] + [full(experts, LANES)] * lists,
            out_shape=[shape_of((rows, columns), BF16)] + [shape_of((experts, LANES), F32)] * lists,
            scratch_shapes=[pltpu.VMEM((rows, HALVES * cap), BF16)],
            compiler_params=params(),
            name="raw_grads",
        )(expert_picks, upstream, weight)
        return out

    def owner_step(got, marks, lists):
        marks_spec = full(experts, LANES) if lists else pl.BlockSpec((rows, LANES), lambda i: (0, half_width // LANES))
        return pl.pallas_call(
            functools.partial(owner_kernel, most, lists),
            grid=(1,),
            in_specs=[pl.BlockSpec((rows, half_width), lambda i: (0, 0)), marks_spec, full(tok_rows, width), full(tok_rows, experts)],
            out_specs=[full(rows, half_width + 2 * LANES), full(rows, LANES), full(tok_rows, experts)],
            out_shape=[
                shape_of((rows, half_width + 2 * LANES), BF16),
                shape_of((rows, LANES), BF16),
                shape_of((tok_rows, experts), BF16),
            ],
            compiler_params=params(),
            name="owner_step",
        )(got, marks, tokens, logits)

    def token_step(got, gated, grad):
        return pl.pallas_call(
            functools.partial(token_kernel, most),
            grid=(1,),
            in_specs=[
                full(1, cap),
                full(rows, half_width),
                full(rows, LANES),
                full(tok_rows, experts),
                full(width, experts),
            ],
            out_specs=[full(tok_rows, width), full(HALVES * cap, rows)],
            out_shape=[shape_of((tok_rows, width), BF16), shape_of((HALVES * cap, rows), BF16)],
            compiler_params=params(32),
            cost_estimate=pl.CostEstimate(flops=10**9, bytes_accessed=4 * 10**6, transcendentals=0),
            name="token_step",
        )(expert_picks, got, gated, grad, router_weight)

    def final_step(got, place):
        chunks = 2
        piece = half_width // chunks
        return pl.pallas_call(
            final_kernel,
            grid=(chunks, HALVES),
            in_specs=[
                pl.BlockSpec((rows, piece), lambda i, h: (0, i)),
                pl.BlockSpec((rows, 2 * LANES), lambda i, h: (0, half_width // (2 * LANES))),
                full(HALVES * cap, rows),
                full(cap, hidden),
            ],
            out_specs=[
                pl.BlockSpec((piece, hidden), lambda i, h: (h * chunks + i, 0)),
                full(width // experts, experts),
            ],
            out_shape=[shape_of((width, hidden), BF16), shape_of((width // experts, experts), F32)],
            compiler_params=params(32),
            name="final_step",
        )(got, got, place, upstream)

    def rest(got, marks, lists):
        send, gated, grad = owner_step(got, marks, lists)
        got_rows = exchange(send, experts)
        token_grad, place = token_step(got, gated, grad)
        weight_grad, router_grad = final_step(got_rows, place)
        return token_grad, weight_grad[None], router_grad

    def ids_inside():
        (raw,) = raw_grads(False)
        got = exchange(raw, experts)
        return rest(got, got, False)

    def ids_first():
        raw, named = raw_grads(True)
        lists = exchange(named, experts)
        return rest(exchange(raw, experts), lists, True)

    return lax.cond(lax.axis_index("dp") == 0, ids_inside, ids_first)


def solution(mesh):
    in_specs = (
        P(("dp", "expert"), None),
        P(("dp", "expert"), None),
        P("expert", None, None),
        P(),
        P(("dp", "expert"), None),
        P(("dp", "expert"), None, None),
    )
    out_specs = (
        P(("dp", "expert"), None),
        P(("dp", "expert"), None, None),
        P(("dp", "expert"), None),
    )
    return jax.shard_map(local, mesh=mesh, in_specs=in_specs, out_specs=out_specs, check_vma=False)
```

```python
import functools

import jax
import jax.numpy as jnp
from jax import lax
from jax.experimental import pallas as pl
from jax.experimental.pallas import tpu as pltpu
from jax.sharding import PartitionSpec as P

F32 = jnp.float32
BF16 = jnp.bfloat16
I32 = jnp.int32
LANES = 128
HALVES = 2
SIDES = (8, 4, 4)
STEP = 256

NN = ((1,), (0,))
NT = ((1,), (1,))
TN = ((0,), (0,))


def matmul(a, b, dims):
    return lax.dot_general(a, b, (dims, ((), ())), preferred_element_type=F32)


def iota(shape, dim):
    return lax.broadcasted_iota(I32, shape, dim)


def params(mebibytes=40):
    return pltpu.CompilerParams(vmem_limit_bytes=mebibytes * 1024 * 1024)


def slots_of(wanted, tok_rows, most):
    cap = wanted.shape[1]
    owners = jnp.broadcast_to(wanted // tok_rows, (8, cap))
    lane = iota((8, cap), 1)
    rank = jnp.zeros((8, cap), I32)
    for back in range(1, most):
        same = (pltpu.roll(owners, back, 1) == owners) & (lane >= back)
        rank = rank + same.astype(I32)
    return owners[:1], rank[:1], wanted % tok_rows + 1


def place_rows(rows, wanted, tok_rows, most):
    owners, rank, _ = slots_of(wanted, tok_rows, most)
    first = owners * (HALVES * most) + rank
    target = jnp.concatenate([first + half * most for half in range(HALVES)], axis=1)
    return iota((rows, target.shape[1]), 0) == target


def name_lists(wanted, owners_count, tok_rows, most):
    owners, rank, marks = slots_of(wanted, tok_rows, most)
    cap = owners.shape[1]
    left = jnp.where(iota((owners_count, cap), 0) == owners, marks, 0).astype(F32).astype(BF16)
    right = (iota((LANES, cap), 0) == rank).astype(F32).astype(BF16)
    return matmul(left, right, NT)


def raw_kernel(tok_rows, most, picks_ref, up_ref, weight_ref, out_ref, *rest):
    place_ref = rest[-1]
    step = pl.program_id(0)
    rows, cap = out_ref.shape[0], up_ref.shape[0]
    half_width = weight_ref.shape[1] * pl.num_programs(0)

    @pl.when(step == 0)
    def _():
        wanted = picks_ref[...]
        hot = place_rows(rows, wanted, tok_rows, most)
        place_ref[...] = hot.astype(F32).astype(BF16)
        if len(rest) > 1:
            rest[0][...] = name_lists(wanted, rest[0].shape[0], tok_rows, most)
        else:
            marks = slots_of(wanted, tok_rows, most)[2]
            both = jnp.concatenate([marks] * HALVES, axis=1)
            named = jnp.where(hot, both, 0).astype(F32).astype(BF16)
            ones = jnp.ones((LANES, HALVES * cap), BF16)
            out_ref[:, half_width:] = matmul(named, ones, NT).astype(BF16)

    up = up_ref[...]
    parts = [matmul(up, weight_ref[half], NT).astype(BF16) for half in range(HALVES)]
    columns = pl.ds(pl.multiple_of(step * STEP, STEP), STEP)
    out_ref[:, columns] = matmul(place_ref[...], jnp.concatenate(parts, axis=0), NN).astype(BF16)


def split_halves(gated, most):
    half = iota(gated.shape, 0) // most % HALVES
    return jnp.concatenate(
        [jnp.where(half == h, gated, 0.0).astype(BF16) for h in range(HALVES)], axis=1
    )


def softmax(logits):
    raised = jnp.exp(logits - jnp.max(logits, axis=1, keepdims=True))
    return raised / jnp.sum(raised, axis=1, keepdims=True)


def stacked(tokens):
    half_width = tokens.shape[1] // HALVES
    return jnp.concatenate(
        [tokens[:, h * half_width : (h + 1) * half_width] for h in range(HALVES)], axis=0
    )


def chosen_tokens(most, lists, marks_ref, rows):
    lane = iota((rows, LANES), 1)
    row = iota((rows, LANES), 0)
    of_expert = (row // (HALVES * most) == lane).astype(F32).astype(BF16)
    if lists:
        spread = matmul(of_expert, marks_ref[...].astype(BF16), NN)
        marks = jnp.sum(jnp.where(lane == row % most, spread, 0.0), axis=1, keepdims=True)
    else:
        marks = marks_ref[...].astype(F32)
    return marks == (lane + 1).astype(F32), of_expert


def rows_kernel(most, lists, marks_ref, tokens_ref, logits_ref, send_ref, gated_ref):
    chosen, of_expert = chosen_tokens(most, lists, marks_ref, send_ref.shape[0])
    gates = matmul(of_expert, softmax(logits_ref[...]).astype(BF16), NT)
    gated = jnp.where(chosen, gates, 0.0)
    gated_ref[...] = gated.astype(BF16)
    send_ref[...] = matmul(split_halves(gated, most), stacked(tokens_ref[...]), NN).astype(BF16)


def grads_kernel(most, lists, index_ref, got_ref, marks_ref, tokens_ref, logits_ref, grad_ref, *rest):
    *outs, shares_ref = rest
    rows = got_ref.shape[0]
    chosen, of_expert = chosen_tokens(most, lists, marks_ref, rows)
    probs = softmax(logits_ref[...])
    tokens = tokens_ref[...]
    products = matmul(got_ref[...], stacked(tokens), NT)
    half = iota((rows, LANES), 0) // most % HALVES
    own = products[:, :LANES]
    for h in range(1, HALVES):
        own = jnp.where(half == h, products[:, h * LANES : (h + 1) * LANES], own)
    own = jnp.where(chosen, own, 0.0)
    whole = own + pltpu.roll(own, most, 0)
    gate_grad = jnp.where(half == HALVES - 1, whole, 0.0).astype(BF16)
    score_grad = matmul(gate_grad, of_expert, TN)
    inner_sum = jnp.sum(probs * score_grad, axis=1, keepdims=True)
    logit_grad = (probs * (score_grad - inner_sum)).astype(BF16)
    grad_ref[...] = logit_grad
    shares_ref[...] = matmul(tokens, logit_grad, TN).reshape(shares_ref.shape)
    size = shares_ref.shape[1]
    here = index_ref[0] % size
    for step, out_ref in enumerate(outs):
        out_ref[...] = shares_ref[:, (here + step) % size].astype(BF16)


def sum_kernel(count, stride, index_ref, *rest):
    ins, outs, total_ref = rest[:count], rest[count:-1], rest[-1]
    total = ins[0][...].astype(F32)
    for in_ref in ins[1:]:
        total = total + in_ref[...].astype(F32)
    total_ref[...] = total.reshape(total_ref.shape)
    size = total_ref.shape[1]
    here = index_ref[0] // stride % size
    for step, out_ref in enumerate(outs):
        out_ref[...] = total_ref[:, (here + step) % size]


def token_kernel(most, picks_ref, got_ref, gated_ref, grad_ref, router_ref, out_ref, place_ref):
    half_width = got_ref.shape[1]
    tok_rows = out_ref.shape[0]
    hot = place_rows(got_ref.shape[0], picks_ref[...], tok_rows, most)
    place_ref[...] = hot.astype(F32).T.astype(BF16)
    expert_part = matmul(split_halves(gated_ref[...].astype(F32), most), got_ref[...], TN)
    for h in range(HALVES):
        columns = slice(h * half_width, (h + 1) * half_width)
        router_part = matmul(grad_ref[...], router_ref[columns, :], NT)
        out_ref[:, columns] = (expert_part[h * tok_rows : (h + 1) * tok_rows] + router_part).astype(BF16)


def final_kernel(got_ref, place_ref, up_ref, out_ref):
    cap = up_ref.shape[0]
    picks = pl.ds(pl.multiple_of(pl.program_id(1) * cap, cap), cap)
    picked = matmul(place_ref[picks, :], got_ref[...], NN).astype(BF16)
    out_ref[...] = matmul(picked, up_ref[...], TN).astype(BF16)


def shifted(x, step, side):
    stride = 1
    for later in SIDES[side + 1 :]:
        stride *= later
    count = stride
    for here in SIDES[: side + 1]:
        count *= here
    pairs = []
    for i in range(count):
        at = i // stride % SIDES[side]
        pairs.append((i, i + ((at + step) % SIDES[side] - at) * stride))
    return lax.ppermute(x, "expert", pairs)


def exchange(x, blocks):
    x = x.reshape(blocks, x.shape[0] // blocks, x.shape[1])
    x = lax.all_to_all(x, "expert", split_axis=0, concat_axis=0, tiled=True)
    return x.reshape(-1, x.shape[2])


def local(tokens, logits, weights, router_weight, expert_picks, cotangent):
    experts = lax.axis_size("expert")
    tok_rows, width = tokens.shape
    hidden = weights.shape[2]
    cap = expert_picks.shape[1]
    most = 2 * cap // experts
    rows = experts * most * HALVES
    half_width = width // HALVES
    weight = weights[0].reshape(HALVES, half_width, hidden)
    upstream = cotangent[0]
    full = lambda *shape: pl.BlockSpec(shape, lambda *_: (0,) * len(shape))
    shape_of = jax.ShapeDtypeStruct

    def raw_grads(lists):
        columns = half_width if lists else half_width + LANES
        out = pl.pallas_call(
            functools.partial(raw_kernel, tok_rows, most),
            grid=(half_width // STEP,),
            in_specs=[
                full(1, cap),
                full(cap, hidden),
                pl.BlockSpec((HALVES, STEP, hidden), lambda i: (0, i, 0)),
            ],
            out_specs=[full(rows, columns)] + [full(experts, LANES)] * lists,
            out_shape=[shape_of((rows, columns), BF16)] + [shape_of((experts, LANES), F32)] * lists,
            scratch_shapes=[pltpu.VMEM((rows, HALVES * cap), BF16)],
            compiler_params=params(),
            name="raw_grads",
        )(expert_picks, upstream, weight)
        return out

    def marks_spec(lists):
        if lists:
            return full(experts, LANES)
        return pl.BlockSpec((rows, LANES), lambda i: (0, half_width // LANES))

    def rows_step(marks, lists):
        return pl.pallas_call(
            functools.partial(rows_kernel, most, lists),
            grid=(1,),
            in_specs=[marks_spec(lists), full(tok_rows, width), full(tok_rows, experts)],
            out_specs=[full(rows, half_width), full(rows, LANES)],
            out_shape=[shape_of((rows, half_width), BF16), shape_of((rows, LANES), BF16)],
            compiler_params=params(),
            cost_estimate=pl.CostEstimate(flops=10**9, bytes_accessed=4 * 10**6, transcendentals=0),
            name="rows_step",
        )(marks, tokens, logits)

    scalar = pl.BlockSpec(memory_space=pltpu.SMEM)
    index = lax.axis_index("expert").astype(I32).reshape(1)
    share = width // experts
    z_size, x_size, y_size = SIDES

    def grads_step(got, marks, lists):
        chunk = (z_size * x_size, share, experts)
        return pl.pallas_call(
            functools.partial(grads_kernel, most, lists),
            grid=(1,),
            in_specs=[
                scalar,
                full(rows, half_width),
                marks_spec(lists),
                full(tok_rows, width),
                full(tok_rows, experts),
            ],
            out_specs=[full(tok_rows, experts)] + [full(*chunk)] * y_size,
            out_shape=[shape_of((tok_rows, experts), BF16)] + [shape_of(chunk, BF16)] * y_size,
            scratch_shapes=[pltpu.VMEM((z_size * x_size, y_size, share, experts), F32)],
            compiler_params=params(),
            cost_estimate=pl.CostEstimate(flops=10**9, bytes_accessed=4 * 10**6, transcendentals=0),
            name="grads_step",
        )(index, got, marks, tokens, logits)

    def sum_step(arrays, outer, size, stride):
        return pl.pallas_call(
            functools.partial(sum_kernel, len(arrays), stride),
            in_specs=[scalar] + [pl.BlockSpec(memory_space=pltpu.VMEM)] * len(arrays),
            out_specs=[pl.BlockSpec(memory_space=pltpu.VMEM)] * size,
            out_shape=[shape_of((outer, share, experts), F32)] * size,
            scratch_shapes=[pltpu.VMEM((outer, size, share, experts), F32)],
            name="sum_step",
        )(index, *arrays)

    def sum_shares(chunks):
        chunks = [chunks[0]] + [shifted(chunks[step], step, 2) for step in range(1, y_size)]
        chunks = sum_step(chunks, z_size, x_size, y_size)
        chunks = [chunks[0]] + [shifted(chunks[step], step, 1) for step in range(1, x_size)]
        chunks = sum_step(chunks, 1, z_size, x_size * y_size)
        total = chunks[0]
        for step in range(1, z_size):
            total = total + shifted(chunks[step], step, 0)
        return total[0]

    def token_step(got, gated, grad):
        return pl.pallas_call(
            functools.partial(token_kernel, most),
            grid=(1,),
            in_specs=[
                full(1, cap),
                full(rows, half_width),
                full(rows, LANES),
                full(tok_rows, experts),
                full(width, experts),
            ],
            out_specs=[full(tok_rows, width), full(HALVES * cap, rows)],
            out_shape=[shape_of((tok_rows, width), BF16), shape_of((HALVES * cap, rows), BF16)],
            compiler_params=params(32),
            cost_estimate=pl.CostEstimate(flops=10**9, bytes_accessed=4 * 10**6, transcendentals=0),
            name="token_step",
        )(expert_picks, got, gated, grad, router_weight)

    def final_step(got, place):
        chunks = 2
        piece = half_width // chunks
        return pl.pallas_call(
            final_kernel,
            grid=(chunks, HALVES),
            in_specs=[
                pl.BlockSpec((rows, piece), lambda i, h: (0, i)),
                full(HALVES * cap, rows),
                full(cap, hidden),
            ],
            out_specs=pl.BlockSpec((piece, hidden), lambda i, h: (h * chunks + i, 0)),
            out_shape=shape_of((width, hidden), BF16),
            compiler_params=params(32),
            name="final_step",
        )(got, place, upstream)

    def rest(got, marks, lists):
        send, gated = rows_step(marks, lists)
        got_rows = exchange(send, experts)
        grad, *chunks = grads_step(got, marks, lists)
        router_grad = sum_shares(chunks)
        token_grad, place = token_step(got, gated, grad)
        return token_grad, final_step(got_rows, place)[None], router_grad

    def ids_inside():
        (raw,) = raw_grads(False)
        got = exchange(raw, experts)
        return rest(got, got, False)

    def ids_first():
        raw, named = raw_grads(True)
        lists = exchange(named, experts)
        return rest(exchange(raw, experts), lists, True)

    return lax.cond(lax.axis_index("dp") == 0, ids_inside, ids_first)


def solution(mesh):
    in_specs = (
        P(("dp", "expert"), None),
        P(("dp", "expert"), None),
        P("expert", None, None),
        P(),
        P(("dp", "expert"), None),
        P(("dp", "expert"), None, None),
    )
    out_specs = (
        P(("dp", "expert"), None),
        P(("dp", "expert"), None, None),
        P(("dp", "expert"), None),
    )
    return jax.shard_map(local, mesh=mesh, in_specs=in_specs, out_specs=out_specs, check_vma=False)
```

```python
import functools

import jax
import jax.numpy as jnp
from jax import lax
from jax.experimental import pallas as pl
from jax.experimental.pallas import tpu as pltpu
from jax.sharding import PartitionSpec as P

F32 = jnp.float32
BF16 = jnp.bfloat16
I32 = jnp.int32
LANES = 128
HALVES = 2
STEP = 256

NN = ((1,), (0,))
NT = ((1,), (1,))
TN = ((0,), (0,))


def matmul(a, b, dims):
    return lax.dot_general(a, b, (dims, ((), ())), preferred_element_type=F32)


def iota(shape, dim):
    return lax.broadcasted_iota(I32, shape, dim)


def params(mebibytes=60):
    return pltpu.CompilerParams(vmem_limit_bytes=mebibytes * 1024 * 1024)


def slots_of(wanted, tok_rows, most):
    cap = wanted.shape[1]
    owners = jnp.broadcast_to(wanted // tok_rows, (8, cap))
    lane = iota((8, cap), 1)
    rank = jnp.zeros((8, cap), I32)
    for back in range(1, most):
        same = (pltpu.roll(owners, back, 1) == owners) & (lane >= back)
        rank = rank + same.astype(I32)
    return owners[:1], rank[:1], wanted % tok_rows + 1


def place_rows(rows, wanted, tok_rows, most):
    owners, rank, _ = slots_of(wanted, tok_rows, most)
    first = owners * (HALVES * most) + rank
    target = jnp.concatenate([first + half * most for half in range(HALVES)], axis=1)
    return iota((rows, target.shape[1]), 0) == target


def name_lists(wanted, owners_count, tok_rows, most):
    owners, rank, marks = slots_of(wanted, tok_rows, most)
    cap = owners.shape[1]
    left = jnp.where(iota((owners_count, cap), 0) == owners, marks, 0).astype(F32).astype(BF16)
    right = (iota((LANES, cap), 0) == rank).astype(F32).astype(BF16)
    return matmul(left, right, NT)


def raw_kernel(tok_rows, most, steps, picks_ref, up_ref, weight_ref, out_ref, *rest):
    place_ref, made_ref, sems = rest[-3:]
    step = pl.program_id(0)
    rows, cap = out_ref.shape[0], up_ref.shape[0]
    half_width = steps * STEP

    def sent(columns, at):
        return pltpu.make_async_copy(made_ref.at[:, columns], out_ref.at[:, columns], sems.at[at])

    def block(at):
        return pl.ds(pl.multiple_of(at * STEP, STEP), STEP)

    @pl.when(step == 0)
    def _():
        wanted = picks_ref[...]
        hot = place_rows(rows, wanted, tok_rows, most)
        place_ref[...] = hot.astype(F32).astype(BF16)
        if len(rest) > 3:
            rest[0][...] = name_lists(wanted, rest[0].shape[0], tok_rows, most)
        else:
            marks = slots_of(wanted, tok_rows, most)[2]
            both = jnp.concatenate([marks] * HALVES, axis=1)
            named = jnp.where(hot, both, 0).astype(F32).astype(BF16)
            ones = jnp.ones((LANES, HALVES * cap), BF16)
            made_ref[:, half_width:] = matmul(named, ones, NT).astype(BF16)
            sent(pl.ds(half_width, LANES), steps).start()

    up = up_ref[...]
    parts = [matmul(up, weight_ref[half], NT).astype(BF16) for half in range(HALVES)]
    raw = matmul(place_ref[...], jnp.concatenate(parts, axis=0), NN)
    made_ref[:, block(step)] = raw.astype(BF16)
    sent(block(step), step).start()

    @pl.when(step == steps - 1)
    def _():
        for at in range(steps):
            sent(block(at), at).wait()
        if made_ref.shape[1] > half_width:
            sent(pl.ds(half_width, LANES), steps).wait()


def split_halves(gated, most):
    half = iota(gated.shape, 0) // most % HALVES
    return jnp.concatenate(
        [jnp.where(half == h, gated, 0.0).astype(BF16) for h in range(HALVES)], axis=1
    )


def owner_kernel(most, lists, raw_ref, marks_ref, tokens_ref, logits_ref, out_ref, *rest):
    gated_ref, grad_ref, got_ref, send_ref, sems = rest
    rows, half_width = got_ref.shape
    fetch = pltpu.make_async_copy(raw_ref.at[:, pl.ds(0, half_width)], got_ref, sems.at[2])
    fetch.start()
    lane = iota((rows, LANES), 1)
    row = iota((rows, LANES), 0)
    of_expert = (row // (HALVES * most) == lane).astype(F32).astype(BF16)
    if lists:
        spread = matmul(of_expert, marks_ref[...].astype(BF16), NN)
        marks = jnp.sum(jnp.where(lane == row % most, spread, 0.0), axis=1, keepdims=True)
    else:
        marks = marks_ref[...].astype(F32)
    chosen = marks == (lane + 1).astype(F32)

    logits = logits_ref[...]
    raised = jnp.exp(logits - jnp.max(logits, axis=1, keepdims=True))
    probs = raised / jnp.sum(raised, axis=1, keepdims=True)
    gates = matmul(of_expert, probs.astype(BF16), NT)
    gated = jnp.where(chosen, gates, 0.0)
    gated_ref[...] = gated.astype(BF16)
    tokens = tokens_ref[...]
    stack = jnp.concatenate(
        [tokens[:, h * half_width : (h + 1) * half_width] for h in range(HALVES)], axis=0
    )
    send_ref[:, :half_width] = matmul(split_halves(gated, most), stack, NN).astype(BF16)
    columns = pl.ds(0, half_width)
    first = pltpu.make_async_copy(send_ref.at[:, columns], out_ref.at[:, columns], sems.at[0])
    first.start()

    fetch.wait()
    products = matmul(got_ref[...], stack, NT)
    half = row // most % HALVES
    own = products[:, :LANES]
    for h in range(1, HALVES):
        own = jnp.where(half == h, products[:, h * LANES : (h + 1) * LANES], own)
    own = jnp.where(chosen, own, 0.0)
    whole = own + pltpu.roll(own, most, 0)
    gate_grad = jnp.where(half == HALVES - 1, whole, 0.0).astype(BF16)
    score_grad = matmul(gate_grad, of_expert, TN)
    inner_sum = jnp.sum(probs * score_grad, axis=1, keepdims=True)
    logit_grad = (probs * (score_grad - inner_sum)).astype(BF16)
    grad_ref[...] = logit_grad
    shares = matmul(tokens, logit_grad, TN)
    blocks = rows // 8
    shares = shares.reshape(blocks, 16, LANES)
    for b in range(2):
        part = shares[:, 8 * b : 8 * (b + 1), :].reshape(rows, LANES)
        send_ref[:, half_width + b * LANES : half_width + (b + 1) * LANES] = part.astype(BF16)
    columns = pl.ds(half_width, 2 * LANES)
    second = pltpu.make_async_copy(send_ref.at[:, columns], out_ref.at[:, columns], sems.at[1])
    second.start()
    first.wait()
    second.wait()


def token_kernel(most, got_ref, gated_ref, grad_ref, router_ref, out_ref):
    half_width = got_ref.shape[1]
    tok_rows = out_ref.shape[0]
    expert_part = matmul(split_halves(gated_ref[...].astype(F32), most), got_ref[...], TN)
    for h in range(HALVES):
        columns = slice(h * half_width, (h + 1) * half_width)
        router_part = matmul(grad_ref[...], router_ref[columns, :], NT)
        out_ref[:, columns] = (expert_part[h * tok_rows : (h + 1) * tok_rows] + router_part).astype(BF16)


def final_kernel(tok_rows, most, got_ref, shares_ref, picks_ref, up_ref, out_ref, router_ref, place_ref):
    rows, cap = got_ref.shape[0], up_ref.shape[0]
    chunk, half = pl.program_id(0), pl.program_id(1)

    @pl.when((chunk == 0) & (half == 0))
    def _():
        hot = place_rows(rows, picks_ref[...], tok_rows, most).astype(F32).astype(BF16)
        for h in range(HALVES):
            place_ref[h] = hot[:, h * cap : (h + 1) * cap]
        for b in range(2):
            part = shares_ref[:, b * LANES : (b + 1) * LANES].astype(F32)
            router_ref[8 * b : 8 * (b + 1), :] = jnp.sum(part.reshape(rows // 8, 8, LANES), axis=0)

    picked = matmul(place_ref[half], got_ref[...], TN).astype(BF16)
    out_ref[...] = matmul(picked, up_ref[...], TN).astype(BF16)


def exchange(x, blocks):
    x = x.reshape(blocks, x.shape[0] // blocks, x.shape[1])
    x = lax.all_to_all(x, "expert", split_axis=0, concat_axis=0, tiled=True)
    return x.reshape(-1, x.shape[2])


def local(tokens, logits, weights, router_weight, expert_picks, cotangent):
    experts = lax.axis_size("expert")
    tok_rows, width = tokens.shape
    hidden = weights.shape[2]
    cap = expert_picks.shape[1]
    most = 2 * cap // experts
    rows = experts * most * HALVES
    half_width = width // HALVES
    weight = weights[0].reshape(HALVES, half_width, hidden)
    upstream = cotangent[0]
    full = lambda *shape: pl.BlockSpec(shape, lambda *_: (0,) * len(shape))
    shape_of = jax.ShapeDtypeStruct

    def raw_grads(lists):
        columns = half_width if lists else half_width + LANES
        out = pl.pallas_call(
            functools.partial(raw_kernel, tok_rows, most, half_width // STEP),
            grid=(half_width // STEP,),
            in_specs=[
                full(1, cap),
                full(cap, hidden),
                pl.BlockSpec((HALVES, STEP, hidden), lambda i: (0, i, 0)),
            ],
            out_specs=[pl.BlockSpec(memory_space=pltpu.HBM)] + [full(experts, LANES)] * lists,
            out_shape=[shape_of((rows, columns), BF16)] + [shape_of((experts, LANES), F32)] * lists,
            scratch_shapes=[
                pltpu.VMEM((rows, HALVES * cap), BF16),
                pltpu.VMEM((rows, columns), BF16),
                pltpu.SemaphoreType.DMA((half_width // STEP + 1,)),
            ],
            compiler_params=params(),
            name="raw_grads",
        )(expert_picks, upstream, weight)
        return out

    def owner_step(got, marks, lists):
        marks_spec = full(experts, LANES) if lists else pl.BlockSpec((rows, LANES), lambda i: (0, half_width // LANES))
        return pl.pallas_call(
            functools.partial(owner_kernel, most, lists),
            grid=(1,),
            in_specs=[pl.BlockSpec(memory_space=pltpu.HBM), marks_spec, full(tok_rows, width), full(tok_rows, experts)],
            out_specs=[pl.BlockSpec(memory_space=pltpu.HBM), full(rows, LANES), full(tok_rows, experts)],
            out_shape=[
                shape_of((rows, half_width + 2 * LANES), BF16),
                shape_of((rows, LANES), BF16),
                shape_of((tok_rows, experts), BF16),
            ],
            scratch_shapes=[
                pltpu.VMEM((rows, half_width), BF16),
                pltpu.VMEM((rows, half_width + 2 * LANES), BF16),
                pltpu.SemaphoreType.DMA((3,)),
            ],
            compiler_params=params(),
            name="owner_step",
        )(got, marks, tokens, logits)

    def token_step(got, gated, grad):
        return pl.pallas_call(
            functools.partial(token_kernel, most),
            grid=(1,),
            in_specs=[full(rows, half_width), full(rows, LANES), full(tok_rows, experts), full(width, experts)],
            out_specs=full(tok_rows, width),
            out_shape=shape_of((tok_rows, width), BF16),
            compiler_params=params(40),
            cost_estimate=pl.CostEstimate(flops=10**9, bytes_accessed=4 * 10**6, transcendentals=0),
            name="token_step",
        )(got, gated, grad, router_weight)

    def final_step(got):
        chunks = 2
        piece = half_width // chunks
        return pl.pallas_call(
            functools.partial(final_kernel, tok_rows, most),
            grid=(chunks, HALVES),
            in_specs=[
                pl.BlockSpec((rows, piece), lambda i, h: (0, i)),
                pl.BlockSpec((rows, 2 * LANES), lambda i, h: (0, half_width // (2 * LANES))),
                full(1, cap),
                full(cap, hidden),
            ],
            out_specs=[
                pl.BlockSpec((piece, hidden), lambda i, h: (h * chunks + i, 0)),
                full(width // experts, experts),
            ],
            out_shape=[shape_of((width, hidden), BF16), shape_of((width // experts, experts), F32)],
            scratch_shapes=[pltpu.VMEM((HALVES, rows, cap), BF16)],
            compiler_params=params(40),
            name="final_step",
        )(got, got, expert_picks, upstream)

    def rest(got, marks, lists):
        send, gated, grad = owner_step(got, marks, lists)
        got_rows = exchange(send, experts)
        token_grad = token_step(got, gated, grad)
        weight_grad, router_grad = final_step(got_rows)
        return token_grad, weight_grad[None], router_grad

    def ids_inside():
        (raw,) = raw_grads(False)
        got = exchange(raw, experts)
        return rest(got, got, False)

    def ids_first():
        raw, named = raw_grads(True)
        lists = exchange(named, experts)
        return rest(exchange(raw, experts), lists, True)

    return lax.cond(lax.axis_index("dp") == 0, ids_inside, ids_first)


def solution(mesh):
    in_specs = (
        P(("dp", "expert"), None),
        P(("dp", "expert"), None),
        P("expert", None, None),
        P(),
        P(("dp", "expert"), None),
        P(("dp", "expert"), None, None),
    )
    out_specs = (
        P(("dp", "expert"), None),
        P(("dp", "expert"), None, None),
        P(("dp", "expert"), None),
    )
    return jax.shard_map(local, mesh=mesh, in_specs=in_specs, out_specs=out_specs, check_vma=False)
```

```python
import functools

import jax
import jax.numpy as jnp
from jax import lax
from jax.experimental import pallas as pl
from jax.experimental.pallas import tpu as pltpu
from jax.sharding import PartitionSpec as P

F32 = jnp.float32
BF16 = jnp.bfloat16
I32 = jnp.int32
LANES = 128
HALVES = 2
STEP = 256

NN = ((1,), (0,))
NT = ((1,), (1,))
TN = ((0,), (0,))


def matmul(a, b, dims):
    return lax.dot_general(a, b, (dims, ((), ())), preferred_element_type=F32)


def iota(shape, dim):
    return lax.broadcasted_iota(I32, shape, dim)


def params(mebibytes=40):
    return pltpu.CompilerParams(vmem_limit_bytes=mebibytes * 1024 * 1024)


def slots_of(wanted, tok_rows, most):
    cap = wanted.shape[1]
    owners = jnp.broadcast_to(wanted // tok_rows, (8, cap))
    lane = iota((8, cap), 1)
    rank = jnp.zeros((8, cap), I32)
    for back in range(1, most):
        same = (pltpu.roll(owners, back, 1) == owners) & (lane >= back)
        rank = rank + same.astype(I32)
    return owners[:1], rank[:1], wanted % tok_rows + 1


def place_rows(rows, wanted, tok_rows, most):
    owners, rank, _ = slots_of(wanted, tok_rows, most)
    first = owners * (HALVES * most) + rank
    target = jnp.concatenate([first + half * most for half in range(HALVES)], axis=1)
    return iota((rows, target.shape[1]), 0) == target


def name_lists(wanted, owners_count, tok_rows, most):
    owners, rank, marks = slots_of(wanted, tok_rows, most)
    cap = owners.shape[1]
    left = jnp.where(iota((owners_count, cap), 0) == owners, marks, 0).astype(F32).astype(BF16)
    right = (iota((LANES, cap), 0) == rank).astype(F32).astype(BF16)
    return matmul(left, right, NT)


def raw_kernel(tok_rows, most, picks_ref, up_ref, weight_ref, out_ref, *rest):
    place_ref = rest[-1]
    step = pl.program_id(0)
    rows, cap = out_ref.shape[0], up_ref.shape[0]
    half_width = weight_ref.shape[1] * pl.num_programs(0)

    @pl.when(step == 0)
    def _():
        wanted = picks_ref[...]
        hot = place_rows(rows, wanted, tok_rows, most)
        place_ref[...] = hot.astype(F32).astype(BF16)
        if len(rest) > 1:
            rest[0][...] = name_lists(wanted, rest[0].shape[0], tok_rows, most)
        else:
            marks = slots_of(wanted, tok_rows, most)[2]
            both = jnp.concatenate([marks] * HALVES, axis=1)
            named = jnp.where(hot, both, 0).astype(F32).astype(BF16)
            ones = jnp.ones((LANES, HALVES * cap), BF16)
            out_ref[:, half_width:] = matmul(named, ones, NT).astype(BF16)

    up = up_ref[...]
    parts = [matmul(up, weight_ref[half], NT).astype(BF16) for half in range(HALVES)]
    columns = pl.ds(pl.multiple_of(step * STEP, STEP), STEP)
    out_ref[:, columns] = matmul(place_ref[...], jnp.concatenate(parts, axis=0), NN).astype(BF16)


def split_halves(gated, most):
    half = iota(gated.shape, 0) // most % HALVES
    return jnp.concatenate(
        [jnp.where(half == h, gated, 0.0).astype(BF16) for h in range(HALVES)], axis=1
    )


def owner_kernel(most, lists, got_ref, marks_ref, tokens_ref, logits_ref, router_ref, send_ref, token_ref):
    rows = send_ref.shape[0]
    half_width = got_ref.shape[1]
    lane = iota((rows, LANES), 1)
    row = iota((rows, LANES), 0)
    of_expert = (row // (HALVES * most) == lane).astype(F32).astype(BF16)
    if lists:
        spread = matmul(of_expert, marks_ref[...].astype(BF16), NN)
        marks = jnp.sum(jnp.where(lane == row % most, spread, 0.0), axis=1, keepdims=True)
    else:
        marks = marks_ref[...].astype(F32)
    chosen = marks == (lane + 1).astype(F32)

    logits = logits_ref[...]
    raised = jnp.exp(logits - jnp.max(logits, axis=1, keepdims=True))
    probs = raised / jnp.sum(raised, axis=1, keepdims=True)
    gates = matmul(of_expert, probs.astype(BF16), NT)
    gated = jnp.where(chosen, gates, 0.0)
    tokens = tokens_ref[...]
    stack = jnp.concatenate(
        [tokens[:, h * half_width : (h + 1) * half_width] for h in range(HALVES)], axis=0
    )
    gated = split_halves(gated, most)
    send_ref[:, :half_width] = matmul(gated, stack, NN).astype(BF16)

    products = matmul(got_ref[...], stack, NT)
    half = row // most % HALVES
    own = products[:, :LANES]
    for h in range(1, HALVES):
        own = jnp.where(half == h, products[:, h * LANES : (h + 1) * LANES], own)
    own = jnp.where(chosen, own, 0.0)
    whole = own + pltpu.roll(own, most, 0)
    gate_grad = jnp.where(half == HALVES - 1, whole, 0.0).astype(BF16)
    score_grad = matmul(gate_grad, of_expert, TN)
    inner_sum = jnp.sum(probs * score_grad, axis=1, keepdims=True)
    logit_grad = (probs * (score_grad - inner_sum)).astype(BF16)
    shares = matmul(tokens, logit_grad, TN)
    blocks = rows // 8
    shares = shares.reshape(blocks, 16, LANES)
    for b in range(2):
        part = shares[:, 8 * b : 8 * (b + 1), :].reshape(rows, LANES)
        send_ref[:, half_width + b * LANES : half_width + (b + 1) * LANES] = part.astype(BF16)

    expert_part = matmul(gated, got_ref[...], TN)
    tok_rows = tokens.shape[0]
    for h in range(HALVES):
        columns = slice(h * half_width, (h + 1) * half_width)
        router_part = matmul(logit_grad, router_ref[columns, :], NT)
        part = expert_part[h * tok_rows : (h + 1) * tok_rows] + router_part
        token_ref[:, columns] = part.astype(BF16)


def final_kernel(tok_rows, most, got_ref, shares_ref, picks_ref, up_ref, out_ref, router_ref, place_ref):
    rows, cap = got_ref.shape[0], up_ref.shape[0]
    chunk, half = pl.program_id(0), pl.program_id(1)

    @pl.when((chunk == 0) & (half == 0))
    def _():
        hot = place_rows(rows, picks_ref[...], tok_rows, most).astype(F32).astype(BF16)
        for h in range(HALVES):
            place_ref[h] = hot[:, h * cap : (h + 1) * cap]
        for b in range(2):
            part = shares_ref[:, b * LANES : (b + 1) * LANES].astype(F32)
            router_ref[8 * b : 8 * (b + 1), :] = jnp.sum(part.reshape(rows // 8, 8, LANES), axis=0)

    picked = matmul(place_ref[half], got_ref[...], TN).astype(BF16)
    out_ref[...] = matmul(picked, up_ref[...], TN).astype(BF16)


def exchange(x, blocks):
    x = x.reshape(blocks, x.shape[0] // blocks, x.shape[1])
    x = lax.all_to_all(x, "expert", split_axis=0, concat_axis=0, tiled=True)
    return x.reshape(-1, x.shape[2])


def local(tokens, logits, weights, router_weight, expert_picks, cotangent):
    experts = lax.axis_size("expert")
    tok_rows, width = tokens.shape
    hidden = weights.shape[2]
    cap = expert_picks.shape[1]
    most = 2 * cap // experts
    rows = experts * most * HALVES
    half_width = width // HALVES
    weight = weights[0].reshape(HALVES, half_width, hidden)
    upstream = cotangent[0]
    full = lambda *shape: pl.BlockSpec(shape, lambda *_: (0,) * len(shape))
    shape_of = jax.ShapeDtypeStruct

    def raw_grads(lists):
        columns = half_width if lists else half_width + LANES
        out = pl.pallas_call(
            functools.partial(raw_kernel, tok_rows, most),
            grid=(half_width // STEP,),
            in_specs=[
                full(1, cap),
                full(cap, hidden),
                pl.BlockSpec((HALVES, STEP, hidden), lambda i: (0, i, 0)),
            ],
            out_specs=[full(rows, columns)] + [full(experts, LANES)] * lists,
            out_shape=[shape_of((rows, columns), BF16)] + [shape_of((experts, LANES), F32)] * lists,
            scratch_shapes=[pltpu.VMEM((rows, HALVES * cap), BF16)],
            compiler_params=params(),
            name="raw_grads",
        )(expert_picks, upstream, weight)
        return out

    def owner_step(got, marks, lists):
        if lists:
            marks_spec = full(experts, LANES)
        else:
            marks_spec = pl.BlockSpec((rows, LANES), lambda i: (0, half_width // LANES))
        return pl.pallas_call(
            functools.partial(owner_kernel, most, lists),
            grid=(1,),
            in_specs=[
                full(rows, half_width),
                marks_spec,
                full(tok_rows, width),
                full(tok_rows, experts),
                full(width, experts),
            ],
            out_specs=[full(rows, half_width + 2 * LANES), full(tok_rows, width)],
            out_shape=[
                shape_of((rows, half_width + 2 * LANES), BF16),
                shape_of((tok_rows, width), BF16),
            ],
            compiler_params=params(),
            name="owner_step",
        )(got, marks, tokens, logits, router_weight)

    def final_step(got):
        chunks = 2
        piece = half_width // chunks
        return pl.pallas_call(
            functools.partial(final_kernel, tok_rows, most),
            grid=(chunks, HALVES),
            in_specs=[
                pl.BlockSpec((rows, piece), lambda i, h: (0, i)),
                pl.BlockSpec((rows, 2 * LANES), lambda i, h: (0, half_width // (2 * LANES))),
                full(1, cap),
                full(cap, hidden),
            ],
            out_specs=[
                pl.BlockSpec((piece, hidden), lambda i, h: (h * chunks + i, 0)),
                full(width // experts, experts),
            ],
            out_shape=[shape_of((width, hidden), BF16), shape_of((width // experts, experts), F32)],
            scratch_shapes=[pltpu.VMEM((HALVES, rows, cap), BF16)],
            compiler_params=params(),
            name="final_step",
        )(got, got, expert_picks, upstream)

    def rest(got, marks, lists):
        send, token_grad = owner_step(got, marks, lists)
        weight_grad, router_grad = final_step(exchange(send, experts))
        return token_grad, weight_grad[None], router_grad

    def ids_inside():
        (raw,) = raw_grads(False)
        got = exchange(raw, experts)
        return rest(got, got, False)

    def ids_first():
        raw, named = raw_grads(True)
        lists = exchange(named, experts)
        return rest(exchange(raw, experts), lists, True)

    return lax.cond(lax.axis_index("dp") == 0, ids_inside, ids_first)


def solution(mesh):
    in_specs = (
        P(("dp", "expert"), None),
        P(("dp", "expert"), None),
        P("expert", None, None),
        P(),
        P(("dp", "expert"), None),
        P(("dp", "expert"), None, None),
    )
    out_specs = (
        P(("dp", "expert"), None),
        P(("dp", "expert"), None, None),
        P(("dp", "expert"), None),
    )
    return jax.shard_map(local, mesh=mesh, in_specs=in_specs, out_specs=out_specs, check_vma=False)
```

```python
import functools

import jax
import jax.numpy as jnp
from jax import lax
from jax.experimental import pallas as pl
from jax.experimental.pallas import tpu as pltpu
from jax.sharding import PartitionSpec as P

F32 = jnp.float32
BF16 = jnp.bfloat16
I32 = jnp.int32
LANES = 128
HALVES = 2
STEP = 512

NN = ((1,), (0,))
NT = ((1,), (1,))
TN = ((0,), (0,))


def matmul(a, b, dims):
    return lax.dot_general(a, b, (dims, ((), ())), preferred_element_type=F32)


def iota(shape, dim):
    return lax.broadcasted_iota(I32, shape, dim)


def params(mebibytes=40):
    return pltpu.CompilerParams(vmem_limit_bytes=mebibytes * 1024 * 1024)


def slots_of(wanted, tok_rows, most):
    cap = wanted.shape[1]
    owners = jnp.broadcast_to(wanted // tok_rows, (8, cap))
    lane = iota((8, cap), 1)
    rank = jnp.zeros((8, cap), I32)
    for back in range(1, most):
        same = (pltpu.roll(owners, back, 1) == owners) & (lane >= back)
        rank = rank + same.astype(I32)
    return owners[:1], rank[:1], wanted % tok_rows + 1


def place_rows(rows, wanted, tok_rows, most):
    owners, rank, _ = slots_of(wanted, tok_rows, most)
    first = owners * (HALVES * most) + rank
    target = jnp.concatenate([first + half * most for half in range(HALVES)], axis=1)
    return iota((rows, target.shape[1]), 0) == target


def name_lists(wanted, owners_count, tok_rows, most):
    owners, rank, marks = slots_of(wanted, tok_rows, most)
    cap = owners.shape[1]
    left = jnp.where(iota((owners_count, cap), 0) == owners, marks, 0).astype(F32).astype(BF16)
    right = (iota((LANES, cap), 0) == rank).astype(F32).astype(BF16)
    return matmul(left, right, NT)


def raw_kernel(tok_rows, most, picks_ref, up_ref, weight_ref, out_ref, *rest):
    place_ref = rest[-1]
    step = pl.program_id(0)
    rows, cap = out_ref.shape[0], up_ref.shape[0]
    half_width = weight_ref.shape[1] * pl.num_programs(0)

    @pl.when(step == 0)
    def _():
        wanted = picks_ref[...]
        hot = place_rows(rows, wanted, tok_rows, most)
        place_ref[...] = hot.astype(F32).astype(BF16)
        if len(rest) > 1:
            rest[0][...] = name_lists(wanted, rest[0].shape[0], tok_rows, most)
        else:
            marks = slots_of(wanted, tok_rows, most)[2]
            both = jnp.concatenate([marks] * HALVES, axis=1)
            named = jnp.where(hot, both, 0).astype(F32).astype(BF16)
            ones = jnp.ones((LANES, HALVES * cap), BF16)
            out_ref[:, half_width:] = matmul(named, ones, NT).astype(BF16)

    up = up_ref[...]
    parts = [matmul(up, weight_ref[half], NT).astype(BF16) for half in range(HALVES)]
    columns = pl.ds(pl.multiple_of(step * STEP, STEP), STEP)
    out_ref[:, columns] = matmul(place_ref[...], jnp.concatenate(parts, axis=0), NN).astype(BF16)


def split_halves(gated, most):
    half = iota(gated.shape, 0) // most % HALVES
    return jnp.concatenate(
        [jnp.where(half == h, gated, 0.0).astype(BF16) for h in range(HALVES)], axis=1
    )


def owner_kernel(most, lists, got_ref, marks_ref, tokens_ref, logits_ref, router_ref, send_ref, token_ref):
    rows = send_ref.shape[0]
    half_width = got_ref.shape[1]
    lane = iota((rows, LANES), 1)
    row = iota((rows, LANES), 0)
    of_expert = (row // (HALVES * most) == lane).astype(F32).astype(BF16)
    if lists:
        spread = matmul(of_expert, marks_ref[...].astype(BF16), NN)
        marks = jnp.sum(jnp.where(lane == row % most, spread, 0.0), axis=1, keepdims=True)
    else:
        marks = marks_ref[...].astype(F32)
    chosen = marks == (lane + 1).astype(F32)

    logits = logits_ref[...]
    raised = jnp.exp(logits - jnp.max(logits, axis=1, keepdims=True))
    probs = raised / jnp.sum(raised, axis=1, keepdims=True)
    gates = matmul(of_expert, probs.astype(BF16), NT)
    gated = jnp.where(chosen, gates, 0.0)
    tokens = tokens_ref[...]
    stack = jnp.concatenate(
        [tokens[:, h * half_width : (h + 1) * half_width] for h in range(HALVES)], axis=0
    )
    gated = split_halves(gated, most)
    send_ref[:, :half_width] = matmul(gated, stack, NN).astype(BF16)

    products = matmul(got_ref[...], stack, NT)
    half = row // most % HALVES
    own = products[:, :LANES]
    for h in range(1, HALVES):
        own = jnp.where(half == h, products[:, h * LANES : (h + 1) * LANES], own)
    own = jnp.where(chosen, own, 0.0)
    whole = own + pltpu.roll(own, most, 0)
    gate_grad = jnp.where(half == HALVES - 1, whole, 0.0).astype(BF16)
    score_grad = matmul(gate_grad, of_expert, TN)
    inner_sum = jnp.sum(probs * score_grad, axis=1, keepdims=True)
    logit_grad = (probs * (score_grad - inner_sum)).astype(BF16)
    shares = matmul(tokens, logit_grad, TN)
    blocks = rows // 8
    shares = shares.reshape(blocks, 16, LANES)
    for b in range(2):
        part = shares[:, 8 * b : 8 * (b + 1), :].reshape(rows, LANES)
        send_ref[:, half_width + b * LANES : half_width + (b + 1) * LANES] = part.astype(BF16)

    expert_part = matmul(gated, got_ref[...], TN)
    tok_rows = tokens.shape[0]
    for h in range(HALVES):
        columns = slice(h * half_width, (h + 1) * half_width)
        router_part = matmul(logit_grad, router_ref[columns, :], NT)
        part = expert_part[h * tok_rows : (h + 1) * tok_rows] + router_part
        token_ref[:, columns] = part.astype(BF16)


def final_kernel(tok_rows, most, got_ref, shares_ref, picks_ref, up_ref, out_ref, router_ref, place_ref):
    rows, cap = got_ref.shape[0], up_ref.shape[0]
    chunk, half = pl.program_id(0), pl.program_id(1)

    @pl.when((chunk == 0) & (half == 0))
    def _():
        hot = place_rows(rows, picks_ref[...], tok_rows, most).astype(F32).astype(BF16)
        for h in range(HALVES):
            place_ref[h] = hot[:, h * cap : (h + 1) * cap]
        for b in range(2):
            part = shares_ref[:, b * LANES : (b + 1) * LANES].astype(F32)
            router_ref[8 * b : 8 * (b + 1), :] = jnp.sum(part.reshape(rows // 8, 8, LANES), axis=0)

    picked = matmul(place_ref[half], got_ref[...], TN).astype(BF16)
    out_ref[...] = matmul(picked, up_ref[...], TN).astype(BF16)


def exchange(x, blocks):
    x = x.reshape(blocks, x.shape[0] // blocks, x.shape[1])
    x = lax.all_to_all(x, "expert", split_axis=0, concat_axis=0, tiled=True)
    return x.reshape(-1, x.shape[2])


def local(tokens, logits, weights, router_weight, expert_picks, cotangent):
    experts = lax.axis_size("expert")
    tok_rows, width = tokens.shape
    hidden = weights.shape[2]
    cap = expert_picks.shape[1]
    most = 2 * cap // experts
    rows = experts * most * HALVES
    half_width = width // HALVES
    weight = weights[0].reshape(HALVES, half_width, hidden)
    upstream = cotangent[0]
    full = lambda *shape: pl.BlockSpec(shape, lambda *_: (0,) * len(shape))
    shape_of = jax.ShapeDtypeStruct

    def raw_grads(lists):
        columns = half_width if lists else half_width + LANES
        out = pl.pallas_call(
            functools.partial(raw_kernel, tok_rows, most),
            grid=(half_width // STEP,),
            in_specs=[
                full(1, cap),
                full(cap, hidden),
                pl.BlockSpec((HALVES, STEP, hidden), lambda i: (0, i, 0)),
            ],
            out_specs=[full(rows, columns)] + [full(experts, LANES)] * lists,
            out_shape=[shape_of((rows, columns), BF16)] + [shape_of((experts, LANES), F32)] * lists,
            scratch_shapes=[pltpu.VMEM((rows, HALVES * cap), BF16)],
            compiler_params=params(),
            name="raw_grads",
        )(expert_picks, upstream, weight)
        return out

    def owner_step(got, marks, lists):
        if lists:
            marks_spec = full(experts, LANES)
        else:
            marks_spec = pl.BlockSpec((rows, LANES), lambda i: (0, half_width // LANES))
        return pl.pallas_call(
            functools.partial(owner_kernel, most, lists),
            grid=(1,),
            in_specs=[
                full(rows, half_width),
                marks_spec,
                full(tok_rows, width),
                full(tok_rows, experts),
                full(width, experts),
            ],
            out_specs=[full(rows, half_width + 2 * LANES), full(tok_rows, width)],
            out_shape=[
                shape_of((rows, half_width + 2 * LANES), BF16),
                shape_of((tok_rows, width), BF16),
            ],
            compiler_params=params(),
            name="owner_step",
        )(got, marks, tokens, logits, router_weight)

    def final_step(got):
        chunks = 1
        piece = half_width // chunks
        return pl.pallas_call(
            functools.partial(final_kernel, tok_rows, most),
            grid=(chunks, HALVES),
            in_specs=[
                pl.BlockSpec((rows, piece), lambda i, h: (0, i)),
                pl.BlockSpec((rows, 2 * LANES), lambda i, h: (0, half_width // (2 * LANES))),
                full(1, cap),
                full(cap, hidden),
            ],
            out_specs=[
                pl.BlockSpec((piece, hidden), lambda i, h: (h * chunks + i, 0)),
                full(width // experts, experts),
            ],
            out_shape=[shape_of((width, hidden), BF16), shape_of((width // experts, experts), F32)],
            scratch_shapes=[pltpu.VMEM((HALVES, rows, cap), BF16)],
            compiler_params=params(),
            name="final_step",
        )(got, got, expert_picks, upstream)

    def rest(got, marks, lists):
        send, token_grad = owner_step(got, marks, lists)
        weight_grad, router_grad = final_step(exchange(send, experts))
        return token_grad, weight_grad[None], router_grad

    def ids_inside():
        (raw,) = raw_grads(False)
        got = exchange(raw, experts)
        return rest(got, got, False)

    def ids_first():
        raw, named = raw_grads(True)
        lists = exchange(named, experts)
        return rest(exchange(raw, experts), lists, True)

    return lax.cond(lax.axis_index("dp") == 0, ids_inside, ids_first)


def solution(mesh):
    in_specs = (
        P(("dp", "expert"), None),
        P(("dp", "expert"), None),
        P("expert", None, None),
        P(),
        P(("dp", "expert"), None),
        P(("dp", "expert"), None, None),
    )
    out_specs = (
        P(("dp", "expert"), None),
        P(("dp", "expert"), None, None),
        P(("dp", "expert"), None),
    )
    return jax.shard_map(local, mesh=mesh, in_specs=in_specs, out_specs=out_specs, check_vma=False)
```

```python
import functools

import jax
import jax.numpy as jnp
from jax import lax
from jax.experimental import pallas as pl
from jax.experimental.pallas import tpu as pltpu
from jax.sharding import PartitionSpec as P

F32 = jnp.float32
BF16 = jnp.bfloat16
I32 = jnp.int32
LANES = 128
HALVES = 2
STEP = 512

NN = ((1,), (0,))
NT = ((1,), (1,))
TN = ((0,), (0,))


def matmul(a, b, dims):
    return lax.dot_general(a, b, (dims, ((), ())), preferred_element_type=F32)


def iota(shape, dim):
    return lax.broadcasted_iota(I32, shape, dim)


def params(mebibytes=40):
    return pltpu.CompilerParams(vmem_limit_bytes=mebibytes * 1024 * 1024)


def slots_of(wanted, tok_rows, most):
    cap = wanted.shape[1]
    owners = jnp.broadcast_to(wanted // tok_rows, (8, cap))
    lane = iota((8, cap), 1)
    rank = jnp.zeros((8, cap), I32)
    for back in range(1, most):
        same = (pltpu.roll(owners, back, 1) == owners) & (lane >= back)
        rank = rank + same.astype(I32)
    return owners[:1], rank[:1], wanted % tok_rows + 1


def place_rows(rows, wanted, tok_rows, most):
    owners, rank, _ = slots_of(wanted, tok_rows, most)
    first = owners * (HALVES * most) + rank
    target = jnp.concatenate([first + half * most for half in range(HALVES)], axis=1)
    return iota((rows, target.shape[1]), 0) == target


def name_lists(wanted, owners_count, tok_rows, most):
    owners, rank, marks = slots_of(wanted, tok_rows, most)
    cap = owners.shape[1]
    left = jnp.where(iota((owners_count, cap), 0) == owners, marks, 0).astype(F32).astype(BF16)
    right = (iota((LANES, cap), 0) == rank).astype(F32).astype(BF16)
    return matmul(left, right, NT)


def raw_kernel(tok_rows, most, picks_ref, up_ref, weight_ref, out_ref, *rest):
    place_ref = rest[-1]
    step = pl.program_id(0)
    rows, cap = out_ref.shape[0], up_ref.shape[0]
    half_width = weight_ref.shape[1] * pl.num_programs(0)

    @pl.when(step == 0)
    def _():
        wanted = picks_ref[...]
        hot = place_rows(rows, wanted, tok_rows, most)
        place_ref[...] = hot.astype(F32).astype(BF16)
        if len(rest) > 1:
            rest[0][...] = name_lists(wanted, rest[0].shape[0], tok_rows, most)
        else:
            marks = slots_of(wanted, tok_rows, most)[2]
            both = jnp.concatenate([marks] * HALVES, axis=1)
            named = jnp.where(hot, both, 0).astype(F32).astype(BF16)
            ones = jnp.ones((LANES, HALVES * cap), BF16)
            out_ref[:, half_width:] = matmul(named, ones, NT).astype(BF16)

    up = up_ref[...]
    parts = [matmul(up, weight_ref[half], NT).astype(BF16) for half in range(HALVES)]
    columns = pl.ds(pl.multiple_of(step * STEP, STEP), STEP)
    out_ref[:, columns] = matmul(place_ref[...], jnp.concatenate(parts, axis=0), NN).astype(BF16)


def split_halves(gated, most):
    half = iota(gated.shape, 0) // most % HALVES
    return jnp.concatenate(
        [jnp.where(half == h, gated, 0.0).astype(BF16) for h in range(HALVES)], axis=1
    )


def softmax(logits):
    raised = jnp.exp(logits - jnp.max(logits, axis=1, keepdims=True))
    return raised / jnp.sum(raised, axis=1, keepdims=True)


def stacked(tokens):
    half_width = tokens.shape[1] // HALVES
    return jnp.concatenate(
        [tokens[:, h * half_width : (h + 1) * half_width] for h in range(HALVES)], axis=0
    )


def experts_of(rows, most):
    hot = iota((rows, LANES), 0) // (HALVES * most) == iota((rows, LANES), 1)
    return hot.astype(F32).astype(BF16)


def gated_tokens(most, chosen, probs):
    of_expert = experts_of(chosen.shape[0], most)
    gates = matmul(of_expert, probs.astype(BF16), NT)
    return split_halves(jnp.where(chosen, gates, 0.0), most)


def gradients(most, chosen, probs, tokens, got):
    rows = got.shape[0]
    products = matmul(got, stacked(tokens), NT)
    half = iota((rows, LANES), 0) // most % HALVES
    own = products[:, :LANES]
    for h in range(1, HALVES):
        own = jnp.where(half == h, products[:, h * LANES : (h + 1) * LANES], own)
    own = jnp.where(chosen, own, 0.0)
    whole = own + pltpu.roll(own, most, 0)
    gate_grad = jnp.where(half == HALVES - 1, whole, 0.0).astype(BF16)
    score_grad = matmul(gate_grad, experts_of(rows, most), TN)
    inner_sum = jnp.sum(probs * score_grad, axis=1, keepdims=True)
    logit_grad = (probs * (score_grad - inner_sum)).astype(BF16)
    shares = matmul(tokens, logit_grad, TN).reshape(rows // 8, 16, LANES)
    parts = [shares[:, 8 * b : 8 * (b + 1), :].reshape(rows, LANES).astype(BF16) for b in range(2)]
    return logit_grad, parts


def token_grads(got, gated, logit_grad, router_ref, token_ref):
    half_width = got.shape[1]
    tok_rows = token_ref.shape[0]
    expert_part = matmul(gated, got, TN)
    for h in range(HALVES):
        columns = slice(h * half_width, (h + 1) * half_width)
        router_part = matmul(logit_grad, router_ref[columns, :], NT)
        part = expert_part[h * tok_rows : (h + 1) * tok_rows] + router_part
        token_ref[:, columns] = part.astype(BF16)


def owner_kernel(most, got_ref, marks_ref, tokens_ref, logits_ref, send_ref, gated_ref, grad_ref):
    rows, half_width = got_ref.shape
    chosen = marks_ref[...].astype(F32) == (iota((rows, LANES), 1) + 1).astype(F32)
    probs = softmax(logits_ref[...])
    tokens = tokens_ref[...]
    gated = gated_tokens(most, chosen, probs)
    gated_ref[...] = gated
    send_ref[:, :half_width] = matmul(gated, stacked(tokens), NN).astype(BF16)
    logit_grad, parts = gradients(most, chosen, probs, tokens, got_ref[...])
    grad_ref[...] = logit_grad
    for b, part in enumerate(parts):
        send_ref[:, half_width + b * LANES : half_width + (b + 1) * LANES] = part


def rows_kernel(most, lists_ref, tokens_ref, logits_ref, send_ref, gated_ref, chosen_ref):
    rows = send_ref.shape[0]
    lane = iota((rows, LANES), 1)
    spread = matmul(experts_of(rows, most), lists_ref[...].astype(BF16), NN)
    slot = lane == iota((rows, LANES), 0) % most
    marks = jnp.sum(jnp.where(slot, spread, 0.0), axis=1, keepdims=True)
    chosen = marks == (lane + 1).astype(F32)
    chosen_ref[...] = chosen.astype(F32).astype(BF16)
    gated = gated_tokens(most, chosen, softmax(logits_ref[...]))
    gated_ref[...] = gated
    send_ref[...] = matmul(gated, stacked(tokens_ref[...]), NN).astype(BF16)


def grads_kernel(most, *refs):
    got_ref, _, gated_ref, chosen_ref, tokens_ref, logits_ref, router_ref, shares_ref, token_ref = refs
    chosen = chosen_ref[...].astype(F32) > 0.5
    probs = softmax(logits_ref[...])
    got = got_ref[...]
    logit_grad, parts = gradients(most, chosen, probs, tokens_ref[...], got)
    for b, part in enumerate(parts):
        shares_ref[:, b * LANES : (b + 1) * LANES] = part
    token_grads(got, gated_ref[...], logit_grad, router_ref, token_ref)


def final_kernel(tok_rows, most, *refs):
    got_ref, shares_ref, picks_ref, up_ref, *extra = refs
    *extra, place_ref = extra
    if len(extra) > 2:
        raw_ref, gated_ref, grad_ref, weight_ref, out_ref, router_ref, token_ref = extra
    else:
        out_ref, router_ref = extra
    rows, cap = got_ref.shape[0], up_ref.shape[0]
    chunk, half = pl.program_id(0), pl.program_id(1)

    @pl.when((chunk == 0) & (half == 0))
    def _():
        hot = place_rows(rows, picks_ref[...], tok_rows, most).astype(F32).astype(BF16)
        for h in range(HALVES):
            place_ref[h] = hot[:, h * cap : (h + 1) * cap]
        for b in range(2):
            part = shares_ref[:, b * LANES : (b + 1) * LANES].astype(F32)
            router_ref[8 * b : 8 * (b + 1), :] = jnp.sum(part.reshape(rows // 8, 8, LANES), axis=0)

    if len(extra) > 2:

        @pl.when((chunk == 0) & (half == 0))
        def _():
            token_grads(raw_ref[...], gated_ref[...], grad_ref[...], weight_ref, token_ref)

    picked = matmul(place_ref[half], got_ref[...], TN).astype(BF16)
    out_ref[...] = matmul(picked, up_ref[...], TN).astype(BF16)


def exchange(x, blocks):
    x = x.reshape(blocks, x.shape[0] // blocks, x.shape[1])
    x = lax.all_to_all(x, "expert", split_axis=0, concat_axis=0, tiled=True)
    return x.reshape(-1, x.shape[2])


def local(tokens, logits, weights, router_weight, expert_picks, cotangent):
    experts = lax.axis_size("expert")
    tok_rows, width = tokens.shape
    hidden = weights.shape[2]
    cap = expert_picks.shape[1]
    most = 2 * cap // experts
    rows = experts * most * HALVES
    half_width = width // HALVES
    weight = weights[0].reshape(HALVES, half_width, hidden)
    upstream = cotangent[0]
    full = lambda *shape: pl.BlockSpec(shape, lambda *_: (0,) * len(shape))
    shape_of = jax.ShapeDtypeStruct

    def raw_grads(lists):
        columns = half_width if lists else half_width + LANES
        out = pl.pallas_call(
            functools.partial(raw_kernel, tok_rows, most),
            grid=(half_width // STEP,),
            in_specs=[
                full(1, cap),
                full(cap, hidden),
                pl.BlockSpec((HALVES, STEP, hidden), lambda i: (0, i, 0)),
            ],
            out_specs=[full(rows, columns)] + [full(experts, LANES)] * lists,
            out_shape=[shape_of((rows, columns), BF16)] + [shape_of((experts, LANES), F32)] * lists,
            scratch_shapes=[pltpu.VMEM((rows, HALVES * cap), BF16)],
            compiler_params=params(),
            name="raw_grads",
        )(expert_picks, upstream, weight)
        return out

    columns = half_width + 2 * LANES

    def owner_step(got):
        return pl.pallas_call(
            functools.partial(owner_kernel, most),
            grid=(1,),
            in_specs=[
                pl.BlockSpec((rows, half_width), lambda i: (0, 0)),
                pl.BlockSpec((rows, LANES), lambda i: (0, half_width // LANES)),
                full(tok_rows, width),
                full(tok_rows, experts),
            ],
            out_specs=[full(rows, columns), full(rows, HALVES * tok_rows), full(tok_rows, experts)],
            out_shape=[
                shape_of((rows, columns), BF16),
                shape_of((rows, HALVES * tok_rows), BF16),
                shape_of((tok_rows, experts), BF16),
            ],
            compiler_params=params(),
            name="owner_step",
        )(got, got, tokens, logits)

    def rows_step(lists):
        return pl.pallas_call(
            functools.partial(rows_kernel, most),
            grid=(1,),
            in_specs=[full(experts, LANES), full(tok_rows, width), full(tok_rows, experts)],
            out_specs=[
                pl.BlockSpec((rows, half_width), lambda i: (0, 0)),
                full(rows, HALVES * tok_rows),
                full(rows, tok_rows),
            ],
            out_shape=[
                shape_of((rows, columns), BF16),
                shape_of((rows, HALVES * tok_rows), BF16),
                shape_of((rows, tok_rows), BF16),
            ],
            compiler_params=params(),
            name="rows_step",
        )(lists, tokens, logits)

    def grads_step(got, send, gated, chosen):
        return pl.pallas_call(
            functools.partial(grads_kernel, most),
            grid=(1,),
            in_specs=[
                full(rows, half_width),
                pl.BlockSpec(memory_space=pl.ANY),
                full(rows, HALVES * tok_rows),
                full(rows, tok_rows),
                full(tok_rows, width),
                full(tok_rows, experts),
                full(width, experts),
            ],
            out_specs=[
                pl.BlockSpec((rows, 2 * LANES), lambda i: (0, half_width // (2 * LANES))),
                full(tok_rows, width),
            ],
            out_shape=[shape_of((rows, columns), BF16), shape_of((tok_rows, width), BF16)],
            input_output_aliases={1: 0},
            compiler_params=params(),
            name="grads_step",
        )(got, send, gated, chosen, tokens, logits, router_weight)

    def final_step(got, known=()):
        chunks = 1
        piece = half_width // chunks
        return pl.pallas_call(
            functools.partial(final_kernel, tok_rows, most),
            grid=(chunks, HALVES),
            in_specs=[
                pl.BlockSpec((rows, piece), lambda i, h: (0, i)),
                pl.BlockSpec((rows, 2 * LANES), lambda i, h: (0, half_width // (2 * LANES))),
                full(1, cap),
                full(cap, hidden),
            ]
            + [
                full(rows, half_width),
                full(rows, HALVES * tok_rows),
                full(tok_rows, experts),
                full(width, experts),
            ][: len(known)],
            out_specs=[
                pl.BlockSpec((piece, hidden), lambda i, h: (h * chunks + i, 0)),
                full(width // experts, experts),
            ]
            + [full(tok_rows, width)] * bool(known),
            out_shape=[shape_of((width, hidden), BF16), shape_of((width // experts, experts), F32)]
            + [shape_of((tok_rows, width), BF16)] * bool(known),
            scratch_shapes=[pltpu.VMEM((HALVES, rows, cap), BF16)],
            compiler_params=params(),
            name="final_step",
        )(got, got, expert_picks, upstream, *known)

    def ids_inside():
        (raw,) = raw_grads(False)
        got = exchange(raw, experts)
        send, gated, grad = owner_step(got)
        known = (got, gated, grad, router_weight)
        weight_grad, router_grad, token_grad = final_step(exchange(send, experts), known)
        return token_grad, weight_grad[None], router_grad

    def ids_first():
        raw, named = raw_grads(True)
        send, gated, chosen = rows_step(exchange(named, experts))
        raw, send = lax.optimization_barrier((raw, send))
        send, token_grad = grads_step(exchange(raw, experts), send, gated, chosen)
        weight_grad, router_grad = final_step(exchange(send, experts))
        return token_grad, weight_grad[None], router_grad

    return lax.cond(lax.axis_index("dp") == 0, ids_inside, ids_first)


def solution(mesh):
    in_specs = (
        P(("dp", "expert"), None),
        P(("dp", "expert"), None),
        P("expert", None, None),
        P(),
        P(("dp", "expert"), None),
        P(("dp", "expert"), None, None),
    )
    out_specs = (
        P(("dp", "expert"), None),
        P(("dp", "expert"), None, None),
        P(("dp", "expert"), None),
    )
    return jax.shard_map(local, mesh=mesh, in_specs=in_specs, out_specs=out_specs, check_vma=False)
```

```python
import functools

import jax
import jax.numpy as jnp
from jax import lax
from jax.experimental import pallas as pl
from jax.experimental.pallas import tpu as pltpu
from jax.sharding import PartitionSpec as P

F32 = jnp.float32
BF16 = jnp.bfloat16
I32 = jnp.int32
LANES = 128
HALVES = 2
STEP = 512

NN = ((1,), (0,))
NT = ((1,), (1,))
TN = ((0,), (0,))


def matmul(a, b, dims):
    return lax.dot_general(a, b, (dims, ((), ())), preferred_element_type=F32)


def iota(shape, dim):
    return lax.broadcasted_iota(I32, shape, dim)


def params(mebibytes=40):
    return pltpu.CompilerParams(vmem_limit_bytes=mebibytes * 1024 * 1024)


def slots_of(wanted, tok_rows, most):
    cap = wanted.shape[1]
    owners = jnp.broadcast_to(wanted // tok_rows, (8, cap))
    lane = iota((8, cap), 1)
    rank = jnp.zeros((8, cap), I32)
    for back in range(1, most):
        same = (pltpu.roll(owners, back, 1) == owners) & (lane >= back)
        rank = rank + same.astype(I32)
    return owners[:1], rank[:1], wanted % tok_rows + 1


def place_rows(rows, wanted, tok_rows, most):
    owners, rank, _ = slots_of(wanted, tok_rows, most)
    first = owners * (HALVES * most) + rank
    target = jnp.concatenate([first + half * most for half in range(HALVES)], axis=1)
    return iota((rows, target.shape[1]), 0) == target


def name_lists(wanted, owners_count, tok_rows, most):
    owners, rank, marks = slots_of(wanted, tok_rows, most)
    cap = owners.shape[1]
    left = jnp.where(iota((owners_count, cap), 0) == owners, marks, 0).astype(F32).astype(BF16)
    right = (iota((LANES, cap), 0) == rank).astype(F32).astype(BF16)
    return matmul(left, right, NT)


def raw_kernel(tok_rows, most, picks_ref, up_ref, weight_ref, out_ref, place_ref, *rest):
    step = pl.program_id(0)
    rows, cap = out_ref.shape[0], up_ref.shape[0]
    half_width = weight_ref.shape[1] * pl.num_programs(0)

    @pl.when(step == 0)
    def _():
        wanted = picks_ref[...]
        hot = place_rows(rows, wanted, tok_rows, most)
        place_ref[...] = hot.astype(F32).astype(BF16)
        if rest:
            rest[0][...] = name_lists(wanted, rest[0].shape[0], tok_rows, most)
        else:
            marks = slots_of(wanted, tok_rows, most)[2]
            both = jnp.concatenate([marks] * HALVES, axis=1)
            named = jnp.where(hot, both, 0).astype(F32).astype(BF16)
            ones = jnp.ones((LANES, HALVES * cap), BF16)
            out_ref[:, half_width:] = matmul(named, ones, NT).astype(BF16)

    up = up_ref[...]
    parts = [matmul(up, weight_ref[half], NT).astype(BF16) for half in range(HALVES)]
    columns = pl.ds(pl.multiple_of(step * STEP, STEP), STEP)
    out_ref[:, columns] = matmul(place_ref[...], jnp.concatenate(parts, axis=0), NN).astype(BF16)


def split_halves(gated, most):
    half = iota(gated.shape, 0) // most % HALVES
    return jnp.concatenate(
        [jnp.where(half == h, gated, 0.0).astype(BF16) for h in range(HALVES)], axis=1
    )


def softmax(logits):
    raised = jnp.exp(logits - jnp.max(logits, axis=1, keepdims=True))
    return raised / jnp.sum(raised, axis=1, keepdims=True)


def stacked(tokens):
    half_width = tokens.shape[1] // HALVES
    return jnp.concatenate(
        [tokens[:, h * half_width : (h + 1) * half_width] for h in range(HALVES)], axis=0
    )


def experts_of(rows, most):
    hot = iota((rows, LANES), 0) // (HALVES * most) == iota((rows, LANES), 1)
    return hot.astype(F32).astype(BF16)


def gated_tokens(most, chosen, probs):
    of_expert = experts_of(chosen.shape[0], most)
    gates = matmul(of_expert, probs.astype(BF16), NT)
    return split_halves(jnp.where(chosen, gates, 0.0), most)


def gradients(most, chosen, probs, tokens, got):
    rows = got.shape[0]
    products = matmul(got, stacked(tokens), NT)
    half = iota((rows, LANES), 0) // most % HALVES
    own = products[:, :LANES]
    for h in range(1, HALVES):
        own = jnp.where(half == h, products[:, h * LANES : (h + 1) * LANES], own)
    own = jnp.where(chosen, own, 0.0)
    whole = own + pltpu.roll(own, most, 0)
    gate_grad = jnp.where(half == HALVES - 1, whole, 0.0).astype(BF16)
    score_grad = matmul(gate_grad, experts_of(rows, most), TN)
    inner_sum = jnp.sum(probs * score_grad, axis=1, keepdims=True)
    logit_grad = (probs * (score_grad - inner_sum)).astype(BF16)
    shares = matmul(tokens, logit_grad, TN).reshape(rows // 8, 16, LANES)
    parts = [shares[:, 8 * b : 8 * (b + 1), :].reshape(rows, LANES).astype(BF16) for b in range(2)]
    return logit_grad, parts


def token_grads(got, gated, logit_grad, router_ref, token_ref):
    half_width = got.shape[1]
    tok_rows = token_ref.shape[0]
    expert_part = matmul(gated, got, TN)
    for h in range(HALVES):
        columns = slice(h * half_width, (h + 1) * half_width)
        router_part = matmul(logit_grad, router_ref[columns, :], NT)
        part = expert_part[h * tok_rows : (h + 1) * tok_rows] + router_part
        token_ref[:, columns] = part.astype(BF16)


def owner_kernel(most, got_ref, marks_ref, tokens_ref, logits_ref, send_ref, gated_ref, grad_ref):
    rows, half_width = got_ref.shape
    chosen = marks_ref[...].astype(F32) == (iota((rows, LANES), 1) + 1).astype(F32)
    probs = softmax(logits_ref[...])
    tokens = tokens_ref[...]
    gated = gated_tokens(most, chosen, probs)
    gated_ref[...] = gated
    send_ref[:, :half_width] = matmul(gated, stacked(tokens), NN).astype(BF16)
    logit_grad, parts = gradients(most, chosen, probs, tokens, got_ref[...])
    grad_ref[...] = logit_grad
    for b, part in enumerate(parts):
        send_ref[:, half_width + b * LANES : half_width + (b + 1) * LANES] = part


def rows_kernel(most, lists_ref, tokens_ref, logits_ref, send_ref, gated_ref, chosen_ref):
    rows = send_ref.shape[0]
    lane = iota((rows, LANES), 1)
    spread = matmul(experts_of(rows, most), lists_ref[...].astype(BF16), NN)
    slot = lane == iota((rows, LANES), 0) % most
    marks = jnp.sum(jnp.where(slot, spread, 0.0), axis=1, keepdims=True)
    chosen = marks == (lane + 1).astype(F32)
    chosen_ref[...] = chosen.astype(F32).astype(BF16)
    gated = gated_tokens(most, chosen, softmax(logits_ref[...]))
    gated_ref[...] = gated
    send_ref[...] = matmul(gated, stacked(tokens_ref[...]), NN).astype(BF16)


def grads_kernel(most, *refs):
    got_ref, _, gated_ref, chosen_ref, tokens_ref, logits_ref, router_ref, shares_ref, token_ref = refs
    chosen = chosen_ref[...].astype(F32) > 0.5
    probs = softmax(logits_ref[...])
    got = got_ref[...]
    logit_grad, parts = gradients(most, chosen, probs, tokens_ref[...], got)
    for b, part in enumerate(parts):
        shares_ref[:, b * LANES : (b + 1) * LANES] = part
    token_grads(got, gated_ref[...], logit_grad, router_ref, token_ref)


def final_kernel(got_ref, shares_ref, place_ref, up_ref, *refs):
    rows = got_ref.shape[0]

    @pl.when((pl.program_id(0) == 0) & (pl.program_id(1) == 0))
    def _():
        if len(refs) > 2:
            raw_ref, gated_ref, grad_ref, weight_ref, _, _, token_ref = refs
            token_grads(raw_ref[...], gated_ref[...], grad_ref[...], weight_ref, token_ref)
        router_ref = refs[1] if len(refs) == 2 else refs[-2]
        for b in range(2):
            part = shares_ref[:, b * LANES : (b + 1) * LANES].astype(F32)
            router_ref[8 * b : 8 * (b + 1), :] = jnp.sum(part.reshape(rows // 8, 8, LANES), axis=0)

    out_ref = refs[0] if len(refs) == 2 else refs[-3]
    picked = matmul(place_ref[...], got_ref[...], TN).astype(BF16)
    out_ref[...] = matmul(picked, up_ref[...], TN).astype(BF16)


def exchange(x, blocks):
    x = x.reshape(blocks, x.shape[0] // blocks, x.shape[1])
    x = lax.all_to_all(x, "expert", split_axis=0, concat_axis=0, tiled=True)
    return x.reshape(-1, x.shape[2])


def local(tokens, logits, weights, router_weight, expert_picks, cotangent):
    experts = lax.axis_size("expert")
    tok_rows, width = tokens.shape
    hidden = weights.shape[2]
    cap = expert_picks.shape[1]
    most = 2 * cap // experts
    rows = experts * most * HALVES
    half_width = width // HALVES
    weight = weights[0].reshape(HALVES, half_width, hidden)
    upstream = cotangent[0]
    full = lambda *shape: pl.BlockSpec(shape, lambda *_: (0,) * len(shape))
    shape_of = jax.ShapeDtypeStruct

    def raw_grads(lists):
        columns = half_width if lists else half_width + LANES
        out = pl.pallas_call(
            functools.partial(raw_kernel, tok_rows, most),
            grid=(half_width // STEP,),
            in_specs=[
                full(1, cap),
                full(cap, hidden),
                pl.BlockSpec((HALVES, STEP, hidden), lambda i: (0, i, 0)),
            ],
            out_specs=[full(rows, columns), full(rows, HALVES * cap)] + [full(experts, LANES)] * lists,
            out_shape=[shape_of((rows, columns), BF16), shape_of((rows, HALVES * cap), BF16)]
            + [shape_of((experts, LANES), F32)] * lists,
            compiler_params=params(),
            name="raw_grads",
        )(expert_picks, upstream, weight)
        return out

    columns = half_width + 2 * LANES

    def owner_step(got):
        return pl.pallas_call(
            functools.partial(owner_kernel, most),
            grid=(1,),
            in_specs=[
                pl.BlockSpec((rows, half_width), lambda i: (0, 0)),
                pl.BlockSpec((rows, LANES), lambda i: (0, half_width // LANES)),
                full(tok_rows, width),
                full(tok_rows, experts),
            ],
            out_specs=[full(rows, columns), full(rows, HALVES * tok_rows), full(tok_rows, experts)],
            out_shape=[
                shape_of((rows, columns), BF16),
                shape_of((rows, HALVES * tok_rows), BF16),
                shape_of((tok_rows, experts), BF16),
            ],
            compiler_params=params(),
            name="owner_step",
        )(got, got, tokens, logits)

    def rows_step(lists):
        return pl.pallas_call(
            functools.partial(rows_kernel, most),
            grid=(1,),
            in_specs=[full(experts, LANES), full(tok_rows, width), full(tok_rows, experts)],
            out_specs=[
                pl.BlockSpec((rows, half_width), lambda i: (0, 0)),
                full(rows, HALVES * tok_rows),
                full(rows, tok_rows),
            ],
            out_shape=[
                shape_of((rows, columns), BF16),
                shape_of((rows, HALVES * tok_rows), BF16),
                shape_of((rows, tok_rows), BF16),
            ],
            compiler_params=params(),
            name="rows_step",
        )(lists, tokens, logits)

    def grads_step(got, send, gated, chosen):
        return pl.pallas_call(
            functools.partial(grads_kernel, most),
            grid=(1,),
            in_specs=[
                full(rows, half_width),
                pl.BlockSpec(memory_space=pl.ANY),
                full(rows, HALVES * tok_rows),
                full(rows, tok_rows),
                full(tok_rows, width),
                full(tok_rows, experts),
                full(width, experts),
            ],
            out_specs=[
                pl.BlockSpec((rows, 2 * LANES), lambda i: (0, half_width // (2 * LANES))),
                full(tok_rows, width),
            ],
            out_shape=[shape_of((rows, columns), BF16), shape_of((tok_rows, width), BF16)],
            input_output_aliases={1: 0},
            compiler_params=params(),
            name="grads_step",
        )(got, send, gated, chosen, tokens, logits, router_weight)

    def final_step(got, place, known=()):
        chunks = 1
        piece = half_width // chunks
        return pl.pallas_call(
            final_kernel,
            grid=(chunks, HALVES),
            in_specs=[
                pl.BlockSpec((rows, piece), lambda i, h: (0, i)),
                pl.BlockSpec((rows, 2 * LANES), lambda i, h: (0, half_width // (2 * LANES))),
                pl.BlockSpec((rows, cap), lambda i, h: (0, h)),
                full(cap, hidden),
            ]
            + [
                full(rows, half_width),
                full(rows, HALVES * tok_rows),
                full(tok_rows, experts),
                full(width, experts),
            ][: len(known)],
            out_specs=[
                pl.BlockSpec((piece, hidden), lambda i, h: (h * chunks + i, 0)),
                full(width // experts, experts),
            ]
            + [full(tok_rows, width)] * bool(known),
            out_shape=[shape_of((width, hidden), BF16), shape_of((width // experts, experts), F32)]
            + [shape_of((tok_rows, width), BF16)] * bool(known),
            compiler_params=params(),
            name="final_step",
        )(got, got, place, upstream, *known)

    def ids_inside():
        raw, place = raw_grads(False)
        got = exchange(raw, experts)
        send, gated, grad = owner_step(got)
        known = (got, gated, grad, router_weight)
        weight_grad, router_grad, token_grad = final_step(exchange(send, experts), place, known)
        return token_grad, weight_grad[None], router_grad

    def ids_first():
        raw, place, named = raw_grads(True)
        send, gated, chosen = rows_step(exchange(named, experts))
        raw, send = lax.optimization_barrier((raw, send))
        send, token_grad = grads_step(exchange(raw, experts), send, gated, chosen)
        weight_grad, router_grad = final_step(exchange(send, experts), place)
        return token_grad, weight_grad[None], router_grad

    return lax.cond(lax.axis_index("dp") == 0, ids_inside, ids_first)


def solution(mesh):
    in_specs = (
        P(("dp", "expert"), None),
        P(("dp", "expert"), None),
        P("expert", None, None),
        P(),
        P(("dp", "expert"), None),
        P(("dp", "expert"), None, None),
    )
    out_specs = (
        P(("dp", "expert"), None),
        P(("dp", "expert"), None, None),
        P(("dp", "expert"), None),
    )
    return jax.shard_map(local, mesh=mesh, in_specs=in_specs, out_specs=out_specs, check_vma=False)
```

```python
import functools

import jax
import jax.numpy as jnp
from jax import lax
from jax.experimental import pallas as pl
from jax.experimental.pallas import tpu as pltpu
from jax.sharding import PartitionSpec as P

F32 = jnp.float32
BF16 = jnp.bfloat16
I32 = jnp.int32
LANES = 128
HALVES = 2
STEP = 512

NN = ((1,), (0,))
NT = ((1,), (1,))
TN = ((0,), (0,))


def matmul(a, b, dims):
    return lax.dot_general(a, b, (dims, ((), ())), preferred_element_type=F32)


def iota(shape, dim):
    return lax.broadcasted_iota(I32, shape, dim)


def params(mebibytes=40):
    return pltpu.CompilerParams(vmem_limit_bytes=mebibytes * 1024 * 1024)


def slots_of(wanted, tok_rows, most):
    cap = wanted.shape[1]
    owners = jnp.broadcast_to(wanted // tok_rows, (8, cap))
    lane = iota((8, cap), 1)
    rank = jnp.zeros((8, cap), I32)
    for back in range(1, most):
        same = (pltpu.roll(owners, back, 1) == owners) & (lane >= back)
        rank = rank + same.astype(I32)
    return owners[:1], rank[:1], wanted % tok_rows + 1


def place_rows(rows, wanted, tok_rows, most):
    owners, rank, _ = slots_of(wanted, tok_rows, most)
    first = owners * (HALVES * most) + rank
    target = jnp.concatenate([first + half * most for half in range(HALVES)], axis=1)
    return iota((rows, target.shape[1]), 0) == target


def lists_kernel(tok_rows, most, picks_ref, out_ref):
    owners, rank, marks = slots_of(picks_ref[...], tok_rows, most)
    cap = owners.shape[1]
    owner = iota((out_ref.shape[0], cap), 0)
    left = jnp.where(owner == owners, marks, 0).astype(F32).astype(BF16)
    right = (iota((LANES, cap), 0) == rank).astype(F32).astype(BF16)
    out_ref[...] = matmul(left, right, NT)


def raw_kernel(tok_rows, most, picks_ref, up_ref, weight_ref, out_ref, place_ref):
    step = pl.program_id(0)
    rows, cap = out_ref.shape[0], up_ref.shape[0]
    half_width = weight_ref.shape[1] * pl.num_programs(0)

    @pl.when(step == 0)
    def _():
        wanted = picks_ref[...]
        hot = place_rows(rows, wanted, tok_rows, most)
        place_ref[...] = hot.astype(F32).astype(BF16)
        if out_ref.shape[1] > half_width:
            marks = slots_of(wanted, tok_rows, most)[2]
            both = jnp.concatenate([marks] * HALVES, axis=1)
            named = jnp.where(hot, both, 0).astype(F32).astype(BF16)
            ones = jnp.ones((LANES, HALVES * cap), BF16)
            out_ref[:, half_width:] = matmul(named, ones, NT).astype(BF16)

    up = up_ref[...]
    parts = [matmul(up, weight_ref[half], NT).astype(BF16) for half in range(HALVES)]
    columns = pl.ds(pl.multiple_of(step * STEP, STEP), STEP)
    out_ref[:, columns] = matmul(place_ref[...], jnp.concatenate(parts, axis=0), NN).astype(BF16)


def split_halves(gated, most):
    half = iota(gated.shape, 0) // most % HALVES
    return jnp.concatenate(
        [jnp.where(half == h, gated, 0.0).astype(BF16) for h in range(HALVES)], axis=1
    )


def softmax(logits):
    raised = jnp.exp(logits - jnp.max(logits, axis=1, keepdims=True))
    return raised / jnp.sum(raised, axis=1, keepdims=True)


def stacked(tokens):
    half_width = tokens.shape[1] // HALVES
    return jnp.concatenate(
        [tokens[:, h * half_width : (h + 1) * half_width] for h in range(HALVES)], axis=0
    )


def experts_of(rows, most):
    hot = iota((rows, LANES), 0) // (HALVES * most) == iota((rows, LANES), 1)
    return hot.astype(F32).astype(BF16)


def gated_tokens(most, chosen, probs):
    of_expert = experts_of(chosen.shape[0], most)
    gates = matmul(of_expert, probs.astype(BF16), NT)
    return split_halves(jnp.where(chosen, gates, 0.0), most)


def gradients(most, chosen, probs, tokens, got):
    rows = got.shape[0]
    products = matmul(got, stacked(tokens), NT)
    half = iota((rows, LANES), 0) // most % HALVES
    own = products[:, :LANES]
    for h in range(1, HALVES):
        own = jnp.where(half == h, products[:, h * LANES : (h + 1) * LANES], own)
    own = jnp.where(chosen, own, 0.0)
    whole = own + pltpu.roll(own, most, 0)
    gate_grad = jnp.where(half == HALVES - 1, whole, 0.0).astype(BF16)
    score_grad = matmul(gate_grad, experts_of(rows, most), TN)
    inner_sum = jnp.sum(probs * score_grad, axis=1, keepdims=True)
    logit_grad = (probs * (score_grad - inner_sum)).astype(BF16)
    shares = matmul(tokens, logit_grad, TN).reshape(rows // 8, 16, LANES)
    parts = [shares[:, 8 * b : 8 * (b + 1), :].reshape(rows, LANES).astype(BF16) for b in range(2)]
    return logit_grad, parts


def token_grads(got, gated, logit_grad, router_ref, token_ref):
    half_width = got.shape[1]
    tok_rows = token_ref.shape[0]
    expert_part = matmul(gated, got, TN)
    for h in range(HALVES):
        columns = slice(h * half_width, (h + 1) * half_width)
        router_part = matmul(logit_grad, router_ref[columns, :], NT)
        part = expert_part[h * tok_rows : (h + 1) * tok_rows] + router_part
        token_ref[:, columns] = part.astype(BF16)


def owner_kernel(most, got_ref, marks_ref, tokens_ref, logits_ref, send_ref, gated_ref, grad_ref):
    rows, half_width = got_ref.shape
    chosen = marks_ref[...].astype(F32) == (iota((rows, LANES), 1) + 1).astype(F32)
    probs = softmax(logits_ref[...])
    tokens = tokens_ref[...]
    gated = gated_tokens(most, chosen, probs)
    gated_ref[...] = gated
    send_ref[:, :half_width] = matmul(gated, stacked(tokens), NN).astype(BF16)
    logit_grad, parts = gradients(most, chosen, probs, tokens, got_ref[...])
    grad_ref[...] = logit_grad
    for b, part in enumerate(parts):
        send_ref[:, half_width + b * LANES : half_width + (b + 1) * LANES] = part


def rows_kernel(most, lists_ref, tokens_ref, logits_ref, send_ref, gated_ref, chosen_ref):
    rows = send_ref.shape[0]
    lane = iota((rows, LANES), 1)
    spread = matmul(experts_of(rows, most), lists_ref[...].astype(BF16), NN)
    slot = lane == iota((rows, LANES), 0) % most
    marks = jnp.sum(jnp.where(slot, spread, 0.0), axis=1, keepdims=True)
    chosen = marks == (lane + 1).astype(F32)
    chosen_ref[...] = chosen.astype(F32).astype(BF16)
    gated = gated_tokens(most, chosen, softmax(logits_ref[...]))
    gated_ref[...] = gated
    send_ref[...] = matmul(gated, stacked(tokens_ref[...]), NN).astype(BF16)


def grads_kernel(most, *refs):
    got_ref, _, gated_ref, chosen_ref, tokens_ref, logits_ref, router_ref, shares_ref, token_ref = refs
    chosen = chosen_ref[...].astype(F32) > 0.5
    probs = softmax(logits_ref[...])
    got = got_ref[...]
    logit_grad, parts = gradients(most, chosen, probs, tokens_ref[...], got)
    for b, part in enumerate(parts):
        shares_ref[:, b * LANES : (b + 1) * LANES] = part
    token_grads(got, gated_ref[...], logit_grad, router_ref, token_ref)


def final_kernel(got_ref, shares_ref, place_ref, up_ref, *refs):
    rows = got_ref.shape[0]

    @pl.when((pl.program_id(0) == 0) & (pl.program_id(1) == 0))
    def _():
        if len(refs) > 2:
            raw_ref, gated_ref, grad_ref, weight_ref, _, _, token_ref = refs
            token_grads(raw_ref[...], gated_ref[...], grad_ref[...], weight_ref, token_ref)
        router_ref = refs[1] if len(refs) == 2 else refs[-2]
        for b in range(2):
            part = shares_ref[:, b * LANES : (b + 1) * LANES].astype(F32)
            router_ref[8 * b : 8 * (b + 1), :] = jnp.sum(part.reshape(rows // 8, 8, LANES), axis=0)

    out_ref = refs[0] if len(refs) == 2 else refs[-3]
    picked = matmul(place_ref[...], got_ref[...], TN).astype(BF16)
    out_ref[...] = matmul(picked, up_ref[...], TN).astype(BF16)


def exchange(x, blocks):
    x = x.reshape(blocks, x.shape[0] // blocks, x.shape[1])
    x = lax.all_to_all(x, "expert", split_axis=0, concat_axis=0, tiled=True)
    return x.reshape(-1, x.shape[2])


def local(tokens, logits, weights, router_weight, expert_picks, cotangent):
    experts = lax.axis_size("expert")
    tok_rows, width = tokens.shape
    hidden = weights.shape[2]
    cap = expert_picks.shape[1]
    most = 2 * cap // experts
    rows = experts * most * HALVES
    half_width = width // HALVES
    weight = weights[0].reshape(HALVES, half_width, hidden)
    upstream = cotangent[0]
    full = lambda *shape: pl.BlockSpec(shape, lambda *_: (0,) * len(shape))
    shape_of = jax.ShapeDtypeStruct

    def raw_grads(columns, picks):
        out = pl.pallas_call(
            functools.partial(raw_kernel, tok_rows, most),
            grid=(half_width // STEP,),
            in_specs=[
                full(1, cap),
                full(cap, hidden),
                pl.BlockSpec((HALVES, STEP, hidden), lambda i: (0, i, 0)),
            ],
            out_specs=[full(rows, columns), full(rows, HALVES * cap)],
            out_shape=[shape_of((rows, columns), BF16), shape_of((rows, HALVES * cap), BF16)],
            compiler_params=params(),
            name="raw_grads",
        )(picks, upstream, weight)
        return out

    columns = half_width + 2 * LANES

    def owner_step(got):
        return pl.pallas_call(
            functools.partial(owner_kernel, most),
            grid=(1,),
            in_specs=[
                pl.BlockSpec((rows, half_width), lambda i: (0, 0)),
                pl.BlockSpec((rows, LANES), lambda i: (0, half_width // LANES)),
                full(tok_rows, width),
                full(tok_rows, experts),
            ],
            out_specs=[full(rows, columns), full(rows, HALVES * tok_rows), full(tok_rows, experts)],
            out_shape=[
                shape_of((rows, columns), BF16),
                shape_of((rows, HALVES * tok_rows), BF16),
                shape_of((tok_rows, experts), BF16),
            ],
            compiler_params=params(),
            name="owner_step",
        )(got, got, tokens, logits)

    def rows_step(lists):
        return pl.pallas_call(
            functools.partial(rows_kernel, most),
            grid=(1,),
            in_specs=[full(experts, LANES), full(tok_rows, width), full(tok_rows, experts)],
            out_specs=[
                pl.BlockSpec((rows, half_width), lambda i: (0, 0)),
                full(rows, HALVES * tok_rows),
                full(rows, tok_rows),
            ],
            out_shape=[
                shape_of((rows, columns), BF16),
                shape_of((rows, HALVES * tok_rows), BF16),
                shape_of((rows, tok_rows), BF16),
            ],
            compiler_params=params(),
            name="rows_step",
        )(lists, tokens, logits)

    def grads_step(got, send, gated, chosen):
        return pl.pallas_call(
            functools.partial(grads_kernel, most),
            grid=(1,),
            in_specs=[
                full(rows, half_width),
                pl.BlockSpec(memory_space=pl.ANY),
                full(rows, HALVES * tok_rows),
                full(rows, tok_rows),
                full(tok_rows, width),
                full(tok_rows, experts),
                full(width, experts),
            ],
            out_specs=[
                pl.BlockSpec((rows, 2 * LANES), lambda i: (0, half_width // (2 * LANES))),
                full(tok_rows, width),
            ],
            out_shape=[shape_of((rows, columns), BF16), shape_of((tok_rows, width), BF16)],
            input_output_aliases={1: 0},
            compiler_params=params(),
            name="grads_step",
        )(got, send, gated, chosen, tokens, logits, router_weight)

    def final_step(got, place, known=()):
        chunks = 1
        piece = half_width // chunks
        return pl.pallas_call(
            final_kernel,
            grid=(chunks, HALVES),
            in_specs=[
                pl.BlockSpec((rows, piece), lambda i, h: (0, i)),
                pl.BlockSpec((rows, 2 * LANES), lambda i, h: (0, half_width // (2 * LANES))),
                pl.BlockSpec((rows, cap), lambda i, h: (0, h)),
                full(cap, hidden),
            ]
            + [
                full(rows, half_width),
                full(rows, HALVES * tok_rows),
                full(tok_rows, experts),
                full(width, experts),
            ][: len(known)],
            out_specs=[
                pl.BlockSpec((piece, hidden), lambda i, h: (h * chunks + i, 0)),
                full(width // experts, experts),
            ]
            + [full(tok_rows, width)] * bool(known),
            out_shape=[shape_of((width, hidden), BF16), shape_of((width // experts, experts), F32)]
            + [shape_of((tok_rows, width), BF16)] * bool(known),
            compiler_params=params(),
            name="final_step",
        )(got, got, place, upstream, *known)

    def ids_inside():
        raw, place = raw_grads(half_width + LANES, expert_picks)
        got = exchange(raw, experts)
        send, gated, grad = owner_step(got)
        known = (got, gated, grad, router_weight)
        weight_grad, router_grad, token_grad = final_step(exchange(send, experts), place, known)
        return token_grad, weight_grad[None], router_grad

    def ids_first():
        named = pl.pallas_call(
            functools.partial(lists_kernel, tok_rows, most),
            out_shape=shape_of((experts, LANES), F32),
            name="lists",
        )(expert_picks)
        send, gated, chosen = rows_step(exchange(named, experts))
        picks, send = lax.optimization_barrier((expert_picks, send))
        raw, place = raw_grads(half_width, picks)
        send, token_grad = grads_step(exchange(raw, experts), send, gated, chosen)
        weight_grad, router_grad = final_step(exchange(send, experts), place)
        return token_grad, weight_grad[None], router_grad

    return lax.cond(lax.axis_index("dp") == 0, ids_inside, ids_first)


def solution(mesh):
    in_specs = (
        P(("dp", "expert"), None),
        P(("dp", "expert"), None),
        P("expert", None, None),
        P(),
        P(("dp", "expert"), None),
        P(("dp", "expert"), None, None),
    )
    out_specs = (
        P(("dp", "expert"), None),
        P(("dp", "expert"), None, None),
        P(("dp", "expert"), None),
    )
    return jax.shard_map(local, mesh=mesh, in_specs=in_specs, out_specs=out_specs, check_vma=False)
```

```python
import functools

import jax
import jax.numpy as jnp
from jax import lax
from jax.experimental import pallas as pl
from jax.experimental.pallas import tpu as pltpu
from jax.sharding import PartitionSpec as P

F32 = jnp.float32
BF16 = jnp.bfloat16
I32 = jnp.int32
LANES = 128
HALVES = 2
PARTS = 2
STEP = 512

NN = ((1,), (0,))
NT = ((1,), (1,))
TN = ((0,), (0,))


def matmul(a, b, dims):
    return lax.dot_general(a, b, (dims, ((), ())), preferred_element_type=F32)


def iota(shape, dim):
    return lax.broadcasted_iota(I32, shape, dim)


def params(mebibytes=40):
    return pltpu.CompilerParams(vmem_limit_bytes=mebibytes * 1024 * 1024)


def slots_of(wanted, tok_rows, most):
    cap = wanted.shape[1]
    owners = jnp.broadcast_to(wanted // tok_rows, (8, cap))
    lane = iota((8, cap), 1)
    rank = jnp.zeros((8, cap), I32)
    for back in range(1, most):
        same = (pltpu.roll(owners, back, 1) == owners) & (lane >= back)
        rank = rank + same.astype(I32)
    return owners[:1], rank[:1], wanted % tok_rows + 1


def place_rows(rows, wanted, tok_rows, most):
    owners, rank, _ = slots_of(wanted, tok_rows, most)
    first = owners * (HALVES * most) + rank
    target = jnp.concatenate([first + half * most for half in range(HALVES)], axis=1)
    return iota((rows, target.shape[1]), 0) == target


def lists_kernel(tok_rows, most, picks_ref, out_ref):
    owners, rank, marks = slots_of(picks_ref[...], tok_rows, most)
    cap = owners.shape[1]
    owner = iota((out_ref.shape[0], cap), 0)
    left = jnp.where(owner == owners, marks, 0).astype(F32).astype(BF16)
    right = (iota((LANES, cap), 0) == rank).astype(F32).astype(BF16)
    out_ref[...] = matmul(left, right, NT)


def raw_kernel(tok_rows, most, picks_ref, up_ref, weight_ref, out_ref, place_ref):
    step = pl.program_id(0)
    rows, cap = out_ref.shape[0], up_ref.shape[0]
    half_width = weight_ref.shape[1] * pl.num_programs(0)

    @pl.when(step == 0)
    def _():
        wanted = picks_ref[...]
        hot = place_rows(rows, wanted, tok_rows, most)
        place_ref[...] = hot.astype(F32).astype(BF16)
        if out_ref.shape[1] > half_width:
            marks = slots_of(wanted, tok_rows, most)[2]
            both = jnp.concatenate([marks] * HALVES, axis=1)
            named = jnp.where(hot, both, 0).astype(F32).astype(BF16)
            ones = jnp.ones((LANES, HALVES * cap), BF16)
            out_ref[:, half_width:] = matmul(named, ones, NT).astype(BF16)

    up = up_ref[...]
    parts = [matmul(up, weight_ref[half], NT).astype(BF16) for half in range(HALVES)]
    columns = pl.ds(pl.multiple_of(step * STEP, STEP), STEP)
    out_ref[:, columns] = matmul(place_ref[...], jnp.concatenate(parts, axis=0), NN).astype(BF16)


def split_halves(gated, most):
    half = iota(gated.shape, 0) // most % HALVES
    return jnp.concatenate(
        [jnp.where(half == h, gated, 0.0).astype(BF16) for h in range(HALVES)], axis=1
    )


def softmax(logits):
    raised = jnp.exp(logits - jnp.max(logits, axis=1, keepdims=True))
    return raised / jnp.sum(raised, axis=1, keepdims=True)


def stacked(tokens):
    half_width = tokens.shape[1] // HALVES
    return jnp.concatenate(
        [tokens[:, h * half_width : (h + 1) * half_width] for h in range(HALVES)], axis=0
    )


def experts_of(rows, most):
    hot = iota((rows, LANES), 0) // (HALVES * most) == iota((rows, LANES), 1)
    return hot.astype(F32).astype(BF16)


def gated_tokens(most, chosen, probs):
    of_expert = experts_of(chosen.shape[0], most)
    gates = matmul(of_expert, probs.astype(BF16), NT)
    return split_halves(jnp.where(chosen, gates, 0.0), most)


def gradients(most, chosen, probs, tokens, got):
    rows = got.shape[0]
    products = matmul(got, stacked(tokens), NT)
    half = iota((rows, LANES), 0) // most % HALVES
    own = products[:, :LANES]
    for h in range(1, HALVES):
        own = jnp.where(half == h, products[:, h * LANES : (h + 1) * LANES], own)
    own = jnp.where(chosen, own, 0.0)
    whole = own + pltpu.roll(own, most, 0)
    gate_grad = jnp.where(half == HALVES - 1, whole, 0.0).astype(BF16)
    score_grad = matmul(gate_grad, experts_of(rows, most), TN)
    inner_sum = jnp.sum(probs * score_grad, axis=1, keepdims=True)
    logit_grad = (probs * (score_grad - inner_sum)).astype(BF16)
    shares = matmul(tokens, logit_grad, TN).reshape(rows // 8, 16, LANES)
    parts = [shares[:, 8 * b : 8 * (b + 1), :].reshape(rows, LANES).astype(BF16) for b in range(2)]
    return logit_grad, parts


def token_grads(got, gated, logit_grad, router_ref, token_ref):
    half_width = got.shape[1]
    tok_rows = token_ref.shape[0]
    expert_part = matmul(gated, got, TN)
    for h in range(HALVES):
        columns = slice(h * half_width, (h + 1) * half_width)
        router_part = matmul(logit_grad, router_ref[columns, :], NT)
        part = expert_part[h * tok_rows : (h + 1) * tok_rows] + router_part
        token_ref[:, columns] = part.astype(BF16)


def owner_kernel(most, got_ref, marks_ref, tokens_ref, logits_ref, send_ref, gated_ref, grad_ref):
    rows, half_width = got_ref.shape
    chosen = marks_ref[...].astype(F32) == (iota((rows, LANES), 1) + 1).astype(F32)
    probs = softmax(logits_ref[...])
    tokens = tokens_ref[...]
    gated = gated_tokens(most, chosen, probs)
    gated_ref[...] = gated
    send_ref[:, :half_width] = matmul(gated, stacked(tokens), NN).astype(BF16)
    logit_grad, parts = gradients(most, chosen, probs, tokens, got_ref[...])
    grad_ref[...] = logit_grad
    for b, part in enumerate(parts):
        send_ref[:, half_width + b * LANES : half_width + (b + 1) * LANES] = part


def rows_kernel(most, lists_ref, tokens_ref, logits_ref, send_ref, gated_ref, chosen_ref):
    rows = send_ref.shape[0]
    lane = iota((rows, LANES), 1)
    spread = matmul(experts_of(rows, most), lists_ref[...].astype(BF16), NN)
    slot = lane == iota((rows, LANES), 0) % most
    marks = jnp.sum(jnp.where(slot, spread, 0.0), axis=1, keepdims=True)
    chosen = marks == (lane + 1).astype(F32)
    chosen_ref[...] = chosen.astype(F32).astype(BF16)
    gated = gated_tokens(most, chosen, softmax(logits_ref[...]))
    gated_ref[...] = gated
    send_ref[...] = matmul(gated, stacked(tokens_ref[...]), NN).astype(BF16)


def grads_kernel(most, *refs):
    got_ref, _, gated_ref, chosen_ref, tokens_ref, logits_ref, router_ref, shares_ref, token_ref = refs
    chosen = chosen_ref[...].astype(F32) > 0.5
    probs = softmax(logits_ref[...])
    got = got_ref[...]
    logit_grad, parts = gradients(most, chosen, probs, tokens_ref[...], got)
    for b, part in enumerate(parts):
        shares_ref[:, b * LANES : (b + 1) * LANES] = part
    token_grads(got, gated_ref[...], logit_grad, router_ref, token_ref)


def final_kernel(got_ref, shares_ref, place_ref, up_ref, *refs):
    *refs, picked_ref = refs
    rows = got_ref.shape[0]

    @pl.when((pl.program_id(0) == 0) & (pl.program_id(1) == 0))
    def _():
        if len(refs) > 2:
            raw_ref, gated_ref, grad_ref, weight_ref, _, _, token_ref = refs
            token_grads(raw_ref[...], gated_ref[...], grad_ref[...], weight_ref, token_ref)
        router_ref = refs[1] if len(refs) == 2 else refs[-2]
        for b in range(2):
            part = shares_ref[:, b * LANES : (b + 1) * LANES].astype(F32)
            router_ref[8 * b : 8 * (b + 1), :] = jnp.sum(part.reshape(rows // 8, 8, LANES), axis=0)

    out_ref = refs[0] if len(refs) == 2 else refs[-3]

    @pl.when(pl.program_id(1) == 0)
    def _():
        picked = matmul(place_ref[...], got_ref[...], TN).astype(BF16)
        for part in range(PARTS):
            size = picked.shape[1] // PARTS
            picked_ref[part] = picked[:, part * size : (part + 1) * size]

    out_ref[...] = matmul(picked_ref[pl.program_id(1)], up_ref[...], TN).astype(BF16)


def exchange(x, blocks):
    x = x.reshape(blocks, x.shape[0] // blocks, x.shape[1])
    x = lax.all_to_all(x, "expert", split_axis=0, concat_axis=0, tiled=True)
    return x.reshape(-1, x.shape[2])


def local(tokens, logits, weights, router_weight, expert_picks, cotangent):
    experts = lax.axis_size("expert")
    tok_rows, width = tokens.shape
    hidden = weights.shape[2]
    cap = expert_picks.shape[1]
    most = 2 * cap // experts
    rows = experts * most * HALVES
    half_width = width // HALVES
    weight = weights[0].reshape(HALVES, half_width, hidden)
    upstream = cotangent[0]
    full = lambda *shape: pl.BlockSpec(shape, lambda *_: (0,) * len(shape))
    shape_of = jax.ShapeDtypeStruct

    def raw_grads(columns, picks):
        out = pl.pallas_call(
            functools.partial(raw_kernel, tok_rows, most),
            grid=(half_width // STEP,),
            in_specs=[
                full(1, cap),
                full(cap, hidden),
                pl.BlockSpec((HALVES, STEP, hidden), lambda i: (0, i, 0)),
            ],
            out_specs=[full(rows, columns), full(rows, HALVES * cap)],
            out_shape=[shape_of((rows, columns), BF16), shape_of((rows, HALVES * cap), BF16)],
            compiler_params=params(),
            name="raw_grads",
        )(picks, upstream, weight)
        return out

    columns = half_width + 2 * LANES

    def owner_step(got):
        return pl.pallas_call(
            functools.partial(owner_kernel, most),
            grid=(1,),
            in_specs=[
                pl.BlockSpec((rows, half_width), lambda i: (0, 0)),
                pl.BlockSpec((rows, LANES), lambda i: (0, half_width // LANES)),
                full(tok_rows, width),
                full(tok_rows, experts),
            ],
            out_specs=[full(rows, columns), full(rows, HALVES * tok_rows), full(tok_rows, experts)],
            out_shape=[
                shape_of((rows, columns), BF16),
                shape_of((rows, HALVES * tok_rows), BF16),
                shape_of((tok_rows, experts), BF16),
            ],
            compiler_params=params(),
            name="owner_step",
        )(got, got, tokens, logits)

    def rows_step(lists):
        return pl.pallas_call(
            functools.partial(rows_kernel, most),
            grid=(1,),
            in_specs=[full(experts, LANES), full(tok_rows, width), full(tok_rows, experts)],
            out_specs=[
                pl.BlockSpec((rows, half_width), lambda i: (0, 0)),
                full(rows, HALVES * tok_rows),
                full(rows, tok_rows),
            ],
            out_shape=[
                shape_of((rows, columns), BF16),
                shape_of((rows, HALVES * tok_rows), BF16),
                shape_of((rows, tok_rows), BF16),
            ],
            compiler_params=params(),
            name="rows_step",
        )(lists, tokens, logits)

    def grads_step(got, send, gated, chosen):
        return pl.pallas_call(
            functools.partial(grads_kernel, most),
            grid=(1,),
            in_specs=[
                full(rows, half_width),
                pl.BlockSpec(memory_space=pl.ANY),
                full(rows, HALVES * tok_rows),
                full(rows, tok_rows),
                full(tok_rows, width),
                full(tok_rows, experts),
                full(width, experts),
            ],
            out_specs=[
                pl.BlockSpec((rows, 2 * LANES), lambda i: (0, half_width // (2 * LANES))),
                full(tok_rows, width),
            ],
            out_shape=[shape_of((rows, columns), BF16), shape_of((tok_rows, width), BF16)],
            input_output_aliases={1: 0},
            compiler_params=params(),
            name="grads_step",
        )(got, send, gated, chosen, tokens, logits, router_weight)

    def final_step(got, place, known=()):
        piece = half_width // PARTS
        return pl.pallas_call(
            final_kernel,
            grid=(HALVES, PARTS),
            in_specs=[
                pl.BlockSpec((rows, half_width), lambda h, i: (0, 0)),
                pl.BlockSpec((rows, 2 * LANES), lambda h, i: (0, half_width // (2 * LANES))),
                pl.BlockSpec((rows, cap), lambda h, i: (0, h)),
                full(cap, hidden),
            ]
            + [
                full(rows, half_width),
                full(rows, HALVES * tok_rows),
                full(tok_rows, experts),
                full(width, experts),
            ][: len(known)],
            out_specs=[
                pl.BlockSpec((piece, hidden), lambda h, i: (h * PARTS + i, 0)),
                full(width // experts, experts),
            ]
            + [full(tok_rows, width)] * bool(known),
            out_shape=[shape_of((width, hidden), BF16), shape_of((width // experts, experts), F32)]
            + [shape_of((tok_rows, width), BF16)] * bool(known),
            scratch_shapes=[pltpu.VMEM((PARTS, cap, piece), BF16)],
            compiler_params=params(),
            name="final_step",
        )(got, got, place, upstream, *known)

    def ids_inside():
        raw, place = raw_grads(half_width + LANES, expert_picks)
        got = exchange(raw, experts)
        send, gated, grad = owner_step(got)
        known = (got, gated, grad, router_weight)
        weight_grad, router_grad, token_grad = final_step(exchange(send, experts), place, known)
        return token_grad, weight_grad[None], router_grad

    def ids_first():
        named = pl.pallas_call(
            functools.partial(lists_kernel, tok_rows, most),
            out_shape=shape_of((experts, LANES), F32),
            name="lists",
        )(expert_picks)
        send, gated, chosen = rows_step(exchange(named, experts))
        picks, send = lax.optimization_barrier((expert_picks, send))
        raw, place = raw_grads(half_width, picks)
        send, token_grad = grads_step(exchange(raw, experts), send, gated, chosen)
        weight_grad, router_grad = final_step(exchange(send, experts), place)
        return token_grad, weight_grad[None], router_grad

    return lax.cond(lax.axis_index("dp") == 0, ids_inside, ids_first)


def solution(mesh):
    in_specs = (
        P(("dp", "expert"), None),
        P(("dp", "expert"), None),
        P("expert", None, None),
        P(),
        P(("dp", "expert"), None),
        P(("dp", "expert"), None, None),
    )
    out_specs = (
        P(("dp", "expert"), None),
        P(("dp", "expert"), None, None),
        P(("dp", "expert"), None),
    )
    return jax.shard_map(local, mesh=mesh, in_specs=in_specs, out_specs=out_specs, check_vma=False)
```
